256 devices in a mesh: dp: 32 (over z, x_hi, core), tensor: 8 (over y, x_lo).
Axes of the slice: x: 4 (x_hi: 2, x_lo: 2; x = x_hi * 2 + x_lo), y: 4, z: 8, core: 2. Of those that a mesh axis runs over, the one named last changes fastest.
Arguments:
- tokens: bfloat16 [24576, 5120], P('dp'), may hold values from -6 to 6
- lengths: int32 [32, 8], P('dp'), may hold values from 1 to 384, 768 in all within a row
- qkv_weight: bfloat16 [5120, 10240], P(('dp', 'tensor')), may hold values from -0.056181208 to 0.056181208
- query_norm_gain: float32 [128], replicated, may hold values from 0.6 to 5
- key_norm_gain: float32 [128], replicated, may hold values from 0.6 to 5
Outputs:
- attended: bfloat16 [24576, 8192], P('dp', 'tensor')
The draws below stay inside these ranges and needn't reach their ends.
All inputs are finite; a program needn't handle non-finite values.
Results may differ from the reference program's by a relative error of at most 0.012.
The reference program's roundings to bfloat16 on the way count: a program that leaves them out, or rounds other values in their place, can miss the bound.
Values may be sent and summed in bfloat16 or wider, within the bound.
No kernel may reach another device: no remote copies, remote signals or barrier semaphores. Data moves between devices by JAX's collectives and lax.ppermute only.
A program may use at most 128 MiB of HBM per device.

```python
import math
import jax
import jax.numpy as jnp
import numpy as np
from jax import lax

MODEL_WIDTH = 5120
QUERY_HEADS = 64
KEY_VALUE_HEADS = 8
HEAD_SIZE = 128
TOK_REP = 768
NREQ = 8
LONGEST = 384
REPLICAS = 32
TOKENS = 24576
QKVW = 10240


def draw_tokens(key, part):
    key = jax.random.fold_in(key, 11)
    key_base, key_scale = jax.random.split(key, 2)
    row_scale = jnp.exp(jax.random.uniform(key_scale, (TOKENS, 1), jnp.float32, math.log(0.3), math.log(3.0)))
    value_rows = jax.random.normal(key_base, (TOKENS, MODEL_WIDTH), jnp.float32) * row_scale
    return jnp.clip(value_rows, -6.0, 6.0).astype(jnp.bfloat16)


def draw_qkv_weight(key, part):
    key = jax.random.fold_in(key, 23)
    value_rows = jnp.clip(jax.random.normal(key, (MODEL_WIDTH, QKVW), jnp.float32), -4.0, 4.0) / math.sqrt(MODEL_WIDTH)
    return value_rows.astype(jnp.bfloat16)


def draw_query_norm_gain(key, part):
    key = jax.random.fold_in(key, 37)
    return jax.random.uniform(key, (HEAD_SIZE,), jnp.float32, 0.6, 1.6)


def draw_key_norm_gain(key, part):
    key = jax.random.fold_in(key, 41)
    return jax.random.uniform(key, (HEAD_SIZE,), jnp.float32, 0.6, 1.6)


def profile(number_of, total, limit, skew):
    portions = [(1 << 20) // math.isqrt(rank ** skew) + 1 for rank in range(2, number_of + 1)]
    surplus, counts = total - limit - (number_of - 1), [1] * (number_of - 1)
    while surplus > 0:
        movable = [i for i in range(number_of - 1) if counts[i] < limit]
        mass, remaining = sum([portions[i] for i in movable]), surplus
        for i in movable:
            more = min(limit - counts[i], max(1, remaining * portions[i] // mass), surplus)
            counts[i] = counts[i] + more
            surplus = surplus - more
    return np.array([limit] + counts)


def ragged(rng, count, total, limit, slope):
    if count == 2:
        one = jax.random.randint(rng, (), max(1, total - limit), min(limit, total - 1) + 1)
        return jnp.stack([one, total - one])
    tallies = jnp.asarray(profile(count, total, limit, slope), jnp.int32)
    twos = (count - 1) // 2
    giver, taker = tallies[1:1 + 2 * twos:2], tallies[2:2 + 2 * twos:2]
    margin = jnp.minimum(giver - 1, limit - taker)
    moved = jax.random.randint(jax.random.fold_in(rng, 1), (twos,), 0, 1 << 20) % (margin + 1)
    tallies = tallies.at[1:1 + 2 * twos:2].set(giver - moved).at[2:2 + 2 * twos:2].set(taker + moved)
    return tallies[jax.random.permutation(jax.random.fold_in(rng, 2), count)]


def setup_inputs(seed: int = 0) -> dict:
    seeds = jax.random.split(jax.random.key(seed), 6)
    tokens = draw_tokens(jax.random.fold_in(seeds[5], 71), 0)
    lengths = jax.vmap(lambda own: ragged(own, NREQ, TOK_REP, LONGEST, 2))(jax.random.split(seeds[1], REPLICAS)).reshape((REPLICAS, NREQ)).astype(jnp.int32)
    qkv_weight = draw_qkv_weight(jax.random.fold_in(seeds[5], 71), 0)
    query_norm_gain = draw_query_norm_gain(jax.random.fold_in(seeds[5], 71), 0)
    key_norm_gain = draw_key_norm_gain(jax.random.fold_in(seeds[5], 71), 0)
    return {"tokens": tokens, "lengths": lengths, "qkv_weight": qkv_weight, "query_norm_gain": query_norm_gain, "key_norm_gain": key_norm_gain}


ROPE_BASE = 1000000.0
NORM_EPS = 1e-06

def request_starts(length_row, row_count):
    ending = jnp.cumsum(length_row)
    offsets = (ending - length_row).astype(jnp.int32)
    row_ids = jnp.arange(row_count, dtype=jnp.int32)
    reached = offsets[None, :] <= row_ids[:, None]
    return lax.optimization_barrier(jnp.max(jnp.where(reached, offsets[None, :], 0), axis=1)).astype(jnp.int32)

def head_norm(field, gain):
    return field * lax.rsqrt(lax.optimization_barrier(jnp.mean(field * field, axis=-1, keepdims=True)) + NORM_EPS) * gain

def rotary(field, token_positions):
    head_width = field.shape[-1]
    half_size = head_width // 2
    frequency = ROPE_BASE ** (-jnp.arange(half_size, dtype=jnp.float32) * 2.0 / head_width)
    angles = token_positions[:, None] * frequency[None, :]
    cosine = jnp.concatenate([jnp.cos(angles), jnp.cos(angles)], axis=1)[:, None, :]
    sine_table = jnp.concatenate([jnp.sin(angles), jnp.sin(angles)], axis=1)[:, None, :]
    front_half = field[..., :half_size]
    back_half = field[..., half_size:]
    turned = jnp.concatenate([-back_half, front_half], axis=-1)
    return field * cosine + turned * sine_table

def divide_heads(query_key_value, q_heads, kv_heads, query_norm_gain, key_norm_gain, token_positions):
    row_count = query_key_value.shape[0]
    head_width = query_norm_gain.shape[0]
    q_end = q_heads * head_width
    k_end = q_end + kv_heads * head_width
    query_rows = query_key_value[:, :q_end].reshape(row_count, q_heads, head_width)
    heads_of_keys = query_key_value[:, q_end:k_end].reshape(row_count, kv_heads, head_width)
    query_rows = rotary(head_norm(query_rows, query_norm_gain), token_positions).astype(jnp.bfloat16)
    heads_of_keys = rotary(head_norm(heads_of_keys, key_norm_gain), token_positions).astype(jnp.bfloat16)
    value_rows = query_key_value[:, k_end:].reshape(row_count, kv_heads, head_width).astype(jnp.bfloat16)
    heads_per_group = q_heads // kv_heads
    query_rows = query_rows.reshape(row_count, kv_heads, heads_per_group, head_width)
    return (query_rows, heads_of_keys, value_rows)

def attend_block(query_rows, heads_of_keys, value_rows, request_start, row_start):
    query_count = query_rows.shape[0]
    key_count = heads_of_keys.shape[0]
    head_width = query_rows.shape[3]
    scores = jnp.einsum('qhgd,khd->hgqk', query_rows.astype(jnp.float32), heads_of_keys.astype(jnp.float32))
    scores = scores * (1.0 / math.sqrt(head_width))
    query_pos = row_start + jnp.arange(query_count, dtype=jnp.int32)
    key_pos = jnp.arange(key_count, dtype=jnp.int32)
    allowed = (key_pos[None, :] <= query_pos[:, None]) & (key_pos[None, :] >= request_start[:, None])
    masked = jnp.where(allowed[None, None], scores, -1e+30)
    row_max = lax.optimization_barrier(jnp.max(masked, axis=3, keepdims=True))
    exponent = jnp.exp(masked - row_max)
    weights = (exponent / lax.optimization_barrier(jnp.sum(exponent, axis=3, keepdims=True))).astype(jnp.bfloat16)
    mixed = jnp.einsum('hgqk,khd->qhgd', weights.astype(jnp.float32), value_rows.astype(jnp.float32))
    return mixed.reshape(query_count, -1).astype(jnp.bfloat16)

def reference(tokens, lengths, qkv_weight, query_norm_gain, key_norm_gain):
    replicas = lengths.shape[0]
    row_count = tokens.shape[0] // replicas
    token_blocks = tokens.reshape(replicas, row_count, tokens.shape[1])

    def one_replica(inputs):
        token_block, length_row = inputs
        query_key_value = jnp.dot(token_block, qkv_weight, preferred_element_type=jnp.float32)
        request_start = request_starts(length_row, row_count)
        token_positions = (jnp.arange(row_count, dtype=jnp.int32) - request_start).astype(jnp.float32)
        query_rows, heads_of_keys, value_rows = divide_heads(query_key_value, QUERY_HEADS, KEY_VALUE_HEADS, query_norm_gain, key_norm_gain, token_positions)
        return attend_block(query_rows, heads_of_keys, value_rows, request_start, 0)
    outputs = lax.map(one_replica, (token_blocks, lengths))
    return outputs.reshape(tokens.shape[0], QUERY_HEADS * HEAD_SIZE)
```

```python
import math

import jax
import jax.numpy as jnp
from jax import lax
from jax.experimental import pallas as pl
from jax.experimental.pallas import tpu as pltpu
from jax.sharding import Mesh, PartitionSpec as P

ROPE_BASE = 1000000.0
NORM_EPS = 1e-06

HEAD = 128
ROWS = 768
WIDTH = 5120
NZ = 8
GROUP = 320
COLS_A = 256
COLS_B = 384
HALF_COLS = COLS_A + COLS_B
TILE = 256
TILES = ROWS // TILE
LONGEST = 384
QBLOCK = 128
TENSOR = ("y", "xl")
UP = [(i, (i + 1) % NZ) for i in range(NZ)]
DOWN = [(i, (i - 1) % NZ) for i in range(NZ)]
SWAP = [(0, 1), (1, 0)]


def request_starts(length_row):
    ending = jnp.cumsum(length_row)
    offsets = ending - length_row
    row_ids = jnp.arange(ROWS, dtype=jnp.int32)
    reached = offsets[None, :] <= row_ids[:, None]
    return jnp.max(jnp.where(reached, offsets[None, :], 0), axis=1)


def rotary_tables(request_start):
    positions = (jnp.arange(ROWS, dtype=jnp.int32) - request_start).astype(jnp.float32)
    half = HEAD // 2
    frequency = ROPE_BASE ** (-jnp.arange(half, dtype=jnp.float32) * 2.0 / HEAD)
    angles = positions[:, None] * frequency[None, :]
    cosine, sine = jnp.cos(angles), jnp.sin(angles)
    return jnp.concatenate([cosine, cosine], axis=1), jnp.concatenate([-sine, sine], axis=1)


def regroup(weight):
    rows = weight.shape[0]
    query = weight[:, :8192].reshape(rows, 8, 2, 512)
    key = weight[:, 8192:9216].reshape(rows, 8, 1, HEAD)
    value = weight[:, 9216:].reshape(rows, 8, 1, HEAD)
    joined = jnp.concatenate([jnp.concatenate([key, value], axis=2), query], axis=3)
    return joined.transpose(2, 1, 0, 3)


def gather_blocks(block):
    part_a, part_b = block[:, :COLS_A], block[:, COLS_A:]
    pieces_a, pieces_b = [], []
    half = GROUP // 2

    other_a = lax.ppermute(part_a, "xh", SWAP)
    up_b = down_b = part_b
    ups, downs = [], []
    for step in range(1, 4):
        up_b = lax.ppermute(up_b, "z", UP)
        down_b = lax.ppermute(down_b, "z", DOWN)
        ups.append(up_b)
        downs.append(down_b)
    last_up = lax.ppermute(up_b[:half], "z", UP)
    last_down = lax.ppermute(down_b[half:], "z", DOWN)
    own = [(part_b, 0, 0, GROUP)]
    for step in range(1, 4):
        own.append((ups[step - 1], -step, 0, GROUP))
        own.append((downs[step - 1], step, 0, GROUP))
    own.append((last_up, 4, 0, half))
    own.append((last_down, 4, half, half))
    for array, offset, first, rows in own:
        pieces_b.append((array, offset, 0, first, rows))
        pieces_b.append((lax.ppermute(array, "xh", SWAP), offset, 1, first, rows))

    pair = jnp.stack([part_a, other_a])
    up_a = down_a = pair
    pieces_a.append((pair, 0, None, 0, GROUP))
    for step in range(1, 4):
        up_a = lax.ppermute(up_a, "z", UP)
        down_a = lax.ppermute(down_a, "z", DOWN)
        pieces_a.append((up_a, -step, None, 0, GROUP))
        pieces_a.append((down_a, step, None, 0, GROUP))
    pieces_a.append((lax.ppermute(up_a[0], "z", UP), 4, 0, 0, GROUP))
    pieces_a.append((lax.ppermute(down_a[1], "z", DOWN), 4, 1, 0, GROUP))
    return pieces_a, pieces_b


def flatten_pieces(pieces):
    arrays, copies = [], []
    for array, offset, flip, first, rows in pieces:
        index = len(arrays)
        arrays.append(array)
        if flip is None:
            copies.append((index, 0, offset, 0, first, rows))
            copies.append((index, 1, offset, 1, first, rows))
        else:
            copies.append((index, None, offset, flip, first, rows))
    return arrays, copies


def project(place, pieces_a, pieces_b, token_sets, cosines, sines, query_gain, key_gain):
    arrays_a, copies_a = flatten_pieces(pieces_a)
    arrays_b, copies_b = flatten_pieces(pieces_b)
    n_a, n_b = len(arrays_a), len(arrays_b)

    def kernel(place_ref, *refs):
        refs_a = refs[:n_a]
        refs_b = refs[n_a : n_a + n_b]
        (tokens_own, tokens_other, cos_ref, sin_ref, qgain_ref, kgain_ref) = refs[n_a + n_b : n_a + n_b + 6]
        out_own, out_other = refs[n_a + n_b + 6 : n_a + n_b + 8]
        weight_a, weight_b, tokens, sem_a, sem_b, sem_t = refs[n_a + n_b + 8 :]
        z, xh, core = place_ref[0], place_ref[1], place_ref[2]

        def weight_copies(sources, copies, target, sems):
            started = []
            for number, (index, lead, offset, flip, first, rows) in enumerate(copies):
                source = sources[index] if lead is None else sources[index].at[lead]
                where = lax.rem(z + (offset + NZ), NZ)
                side = lax.rem(xh + flip, 2)
                started.append(
                    pltpu.make_async_copy(
                        source, target.at[where, side, pl.ds(first, rows)], sems.at[number]
                    )
                )
            return started

        def token_copy(number):
            source = tokens_other if number < TILES else tokens_own
            row = (number % TILES) * TILE
            return pltpu.make_async_copy(
                source.at[pl.ds(row, TILE)], tokens.at[number], sem_t.at[number]
            )

        all_a = weight_copies(refs_a, copies_a, weight_a, sem_a)
        all_b = weight_copies(refs_b, copies_b, weight_b, sem_b)
        for copy in all_a:
            copy.start()
        token_copy(0).start()
        for copy in all_b:
            copy.start()
        for number in range(1, 2 * TILES):
            token_copy(number).start()

        def normed(field, gain, cosine, sine):
            scale = lax.rsqrt(jnp.mean(field * field, axis=1, keepdims=True) + NORM_EPS)
            field = field * scale * gain
            return field * cosine + pltpu.roll(field, HEAD // 2, 1) * sine

        for copy in all_a:
            copy.wait()
        matrix_a = weight_a[...].reshape(WIDTH, COLS_A)
        for number in range(2 * TILES):
            which = 1 if number < TILES else 0
            out_ref = out_other if which else out_own
            rows = pl.ds((number % TILES) * TILE, TILE)
            token_copy(number).wait()
            part = tokens[number]
            cosine, sine = cos_ref[which, rows], sin_ref[which, rows]
            qgain, kgain = qgain_ref[...], kgain_ref[...]
            result = jnp.dot(part, matrix_a, preferred_element_type=jnp.float32)
            raw = result[:, :HEAD]
            key = normed(raw, kgain, cosine, sine)
            out_ref[rows, :HEAD] = jnp.where(core == 0, key, raw).astype(jnp.bfloat16)
            out_ref[rows, HEAD:COLS_A] = normed(result[:, HEAD:], qgain, cosine, sine).astype(
                jnp.bfloat16
            )
            if number == 0:
                for copy in all_b:
                    copy.wait()
            matrix_b = weight_b[...].reshape(WIDTH, COLS_B)
            result = jnp.dot(part, matrix_b, preferred_element_type=jnp.float32)
            for head in range(COLS_B // HEAD):
                field = result[:, head * HEAD : (head + 1) * HEAD]
                out_ref[rows, COLS_A + head * HEAD : COLS_A + (head + 1) * HEAD] = normed(
                    field, qgain, cosine, sine
                ).astype(jnp.bfloat16)

    anywhere = pl.BlockSpec(memory_space=pl.ANY)
    vmem = pl.BlockSpec(memory_space=pltpu.VMEM)
    shape = jax.ShapeDtypeStruct((ROWS, HALF_COLS), jnp.bfloat16)
    return pl.pallas_call(
        kernel,
        out_shape=(shape, shape),
        in_specs=[pl.BlockSpec(memory_space=pltpu.SMEM)] + [anywhere] * (n_a + n_b + 2) + [vmem] * 4,
        out_specs=(vmem, vmem),
        scratch_shapes=[
            pltpu.VMEM((NZ, 2, GROUP, COLS_A), jnp.bfloat16),
            pltpu.VMEM((NZ, 2, GROUP, COLS_B), jnp.bfloat16),
            pltpu.VMEM((2 * TILES, TILE, WIDTH), jnp.bfloat16),
            pltpu.SemaphoreType.DMA((len(copies_a),)),
            pltpu.SemaphoreType.DMA((len(copies_b),)),
            pltpu.SemaphoreType.DMA((2 * TILES,)),
        ],
        compiler_params=pltpu.CompilerParams(vmem_limit_bytes=48 << 20),
        cost_estimate=pl.CostEstimate(
            flops=2 * 2 * ROWS * WIDTH * HALF_COLS, bytes_accessed=24 << 20, transcendentals=0
        ),
        name="project",
    )(place, *arrays_a, *arrays_b, *token_sets, cosines, sines, query_gain, key_gain)


def attend(place, own, received, request_start):
    scale = 1.0 / math.sqrt(HEAD)

    def kernel(place_ref, own_ref, received_ref, start_ref, out_ref, key_ref, value_ref):
        core = place_ref[2]

        @pl.when(core == 0)
        def _():
            key_ref[...] = own_ref[:, :HEAD]
            value_ref[...] = received_ref[:, :HEAD]

        @pl.when(core != 0)
        def _():
            key_ref[...] = received_ref[:, :HEAD]
            value_ref[...] = own_ref[:, :HEAD]

        for block in range(ROWS // QBLOCK):
            rows = pl.ds(block * QBLOCK, QBLOCK)
            low = max(0, block * QBLOCK - LONGEST + 1) // QBLOCK * QBLOCK
            count = (block + 1) * QBLOCK - low
            keys, values = key_ref[pl.ds(low, count)], value_ref[pl.ds(low, count)]
            row_ids = block * QBLOCK + lax.broadcasted_iota(jnp.int32, (QBLOCK, count), 0)
            key_ids = low + lax.broadcasted_iota(jnp.int32, (QBLOCK, count), 1)
            allowed = (key_ids <= row_ids) & (key_ids >= start_ref[rows])
            bias = jnp.where(allowed, 0.0, -1e30)
            for side in range(2):
                source = own_ref if side == 0 else received_ref
                first = pl.multiple_of((core if side == 0 else 1 - core) * 512, 512)
                for head in range(4):
                    queries = source[rows, HEAD + head * HEAD : 2 * HEAD + head * HEAD]
                    scores = lax.dot_general(
                        queries, keys, (((1,), (1,)), ((), ())), preferred_element_type=jnp.float32
                    )
                    scores = scores * scale + bias
                    top = jnp.max(scores, axis=1, keepdims=True)
                    exponent = jnp.exp(scores - top)
                    total = jnp.sum(exponent, axis=1, keepdims=True)
                    weights = (exponent * (1.0 / total)).astype(jnp.bfloat16)
                    mixed = jnp.dot(weights, values, preferred_element_type=jnp.float32)
                    out_ref[rows, pl.ds(first + head * HEAD, HEAD)] = mixed.astype(jnp.bfloat16)

    vmem = pl.BlockSpec(memory_space=pltpu.VMEM)
    return pl.pallas_call(
        kernel,
        out_shape=jax.ShapeDtypeStruct((ROWS, 8 * HEAD), jnp.bfloat16),
        in_specs=[pl.BlockSpec(memory_space=pltpu.SMEM), vmem, vmem, vmem],
        out_specs=vmem,
        scratch_shapes=[
            pltpu.VMEM((ROWS, HEAD), jnp.bfloat16),
            pltpu.VMEM((ROWS, HEAD), jnp.bfloat16),
        ],
        compiler_params=pltpu.CompilerParams(vmem_limit_bytes=32 << 20),
        cost_estimate=pl.CostEstimate(
            flops=4 * 8 * ROWS * 512 * HEAD, bytes_accessed=4 << 20, transcendentals=8 * ROWS * 512
        ),
        name="attend",
    )(place, own, received, request_start)


def shards(tokens, lengths, qkv_weight, query_norm_gain, key_norm_gain):
    place = jnp.stack([lax.axis_index("z"), lax.axis_index("xh"), lax.axis_index("c")]).astype(
        jnp.int32
    )
    other_tokens = lax.ppermute(tokens, "c", SWAP)
    other_lengths = lax.ppermute(lengths, "c", SWAP)

    spread = regroup(qkv_weight).reshape(16, -1, HALF_COLS)
    block = lax.all_to_all(spread, ("c",) + TENSOR, split_axis=0, concat_axis=0, tiled=True)
    block = block.reshape(GROUP, HALF_COLS)

    own_start, other_start = request_starts(lengths[0]), request_starts(other_lengths[0])
    own_cos, own_sin = rotary_tables(own_start)
    other_cos, other_sin = rotary_tables(other_start)
    cosines, sines = jnp.stack([own_cos, other_cos]), jnp.stack([own_sin, other_sin])

    pieces_a, pieces_b = gather_blocks(block)
    own, other = project(
        place,
        pieces_a,
        pieces_b,
        (tokens, other_tokens),
        cosines,
        sines,
        query_norm_gain.reshape(1, HEAD),
        key_norm_gain.reshape(1, HEAD),
    )
    received = lax.ppermute(other, "c", SWAP)
    return attend(place, own, received, own_start.reshape(ROWS, 1))


def solution(mesh):
    fine = Mesh(mesh.devices.reshape(NZ, 2, 2, 4, 2), ("z", "xh", "c") + TENSOR)
    rows = ("z", "xh", "c")
    in_specs = (P(rows, None), P(rows, None), P(rows + TENSOR, None), P(), P())
    return jax.shard_map(
        shards, mesh=fine, in_specs=in_specs, out_specs=P(rows, TENSOR), check_vma=False
    )
```

```python
import math

import jax
import jax.numpy as jnp
from jax import lax
from jax.experimental import pallas as pl
from jax.experimental.pallas import tpu as pltpu
from jax.sharding import Mesh, PartitionSpec as P

ROPE_BASE = 1000000.0
NORM_EPS = 1e-06

HEAD = 128
HEADS = 8
ROWS = 768
NZ = 8
GROUP = 320
DEPTH = 2 * GROUP
COLS = 640
TILE = 256
TILES = ROWS // TILE
LONGEST = 384
QBLOCK = 128
TENSOR = ("y", "xl")
UP = [(z, (z + 1) % NZ) for z in range(NZ)]
DOWN = [(z, (z - 1) % NZ) for z in range(NZ)]
SWAP = [(0, 1), (1, 0)]

ANYWHERE = pl.BlockSpec(memory_space=pl.ANY)
VMEM = pl.BlockSpec(memory_space=pltpu.VMEM)
SMEM = pl.BlockSpec(memory_space=pltpu.SMEM)


def request_starts(length_row):
    ending = jnp.cumsum(length_row)
    offsets = ending - length_row
    row_ids = jnp.arange(ROWS, dtype=jnp.int32)
    reached = offsets[None, :] <= row_ids[:, None]
    return jnp.max(jnp.where(reached, offsets[None, :], 0), axis=1)


def rotary_tables(request_start):
    positions = (jnp.arange(ROWS, dtype=jnp.int32) - request_start).astype(jnp.float32)
    half = HEAD // 2
    frequency = ROPE_BASE ** (-jnp.arange(half, dtype=jnp.float32) * 2.0 / HEAD)
    angles = positions[:, None] * frequency[None, :]
    cosine, sine = jnp.cos(angles), jnp.sin(angles)
    return jnp.concatenate([cosine, cosine], axis=1), jnp.concatenate([-sine, sine], axis=1)


def regroup(weight):
    rows = weight.shape[0]
    query = weight[:, :8192].reshape(rows, 8, 2, 512)
    key = weight[:, 8192:9216].reshape(rows, 8, 1, HEAD)
    value = weight[:, 9216:].reshape(rows, 8, 1, HEAD)
    joined = jnp.concatenate([jnp.concatenate([key, value], axis=2), query], axis=3)
    return joined.transpose(2, 1, 0, 3)


def gather_blocks(block, ahead):
    half = GROUP // 2

    def up(array):
        return lax.ppermute(array, "z", UP)

    def down(array):
        return lax.ppermute(array, "z", DOWN)

    def across(array):
        return lax.ppermute(array, "xh", SWAP)

    up1, down1 = up(block), down(block)
    other = across(block)
    up1, down1, ahead = lax.optimization_barrier((up1, down1, ahead))
    up2, down2 = up(up1), down(down1)
    other_up1, other_down1 = across(up1), across(down1)
    up3, down3 = up(up2), down(down2)
    other_up2, other_down2 = up(other_up1), down(other_down1)
    up4, down4 = up(up3[:half]), down(down3[half:])
    other_up4, other_down4 = across(up4), across(down4)
    other_up3, other_down3 = up(other_up2), down(other_down2)
    early = [
        (block, 0, 0, 0), (other, 0, 1, 0),
        (up1, -1, 0, 0), (other_up1, -1, 1, 0), (down1, 1, 0, 0), (other_down1, 1, 1, 0),
        (up2, -2, 0, 0), (other_up2, -2, 1, 0), (down2, 2, 0, 0), (other_down2, 2, 1, 0),
    ]
    late = [
        (up3, -3, 0, 0), (other_up3, -3, 1, 0), (down3, 3, 0, 0), (other_down3, 3, 1, 0),
        (up4, 4, 0, 0), (down4, 4, 0, half), (other_up4, 4, 1, 0), (other_down4, 4, 1, half),
    ]
    return early, late, ahead


def slots_of(pieces):
    offsets = []
    for _, offset, _, _ in pieces:
        if offset not in offsets:
            offsets.append(offset)
    return offsets


def weight_copies(place_ref, pieces, sources, target, sems):
    offsets = slots_of(pieces)
    copies = [[] for _ in offsets]
    for number, (array, offset, flip, first) in enumerate(pieces):
        slot = offsets.index(offset)
        side = lax.rem(place_ref[1] + flip, 2)
        row = pl.multiple_of(side * GROUP + (slot * DEPTH + first), 16)
        where = target.at[pl.ds(row, array.shape[0])]
        copies[slot].append(pltpu.make_async_copy(sources[number], where, sems.at[number]))
    return copies


def slot_of(offset):
    return (offset + NZ) % NZ


def hold_tokens(place, tokens):
    def kernel(place_ref, token_ref, out_ref, sems):
        copies = [
            pltpu.make_async_copy(
                token_ref.at[
                    :, pl.ds(pl.multiple_of(lax.rem(place_ref[0] + slot, NZ) * DEPTH, HEAD), DEPTH)
                ],
                out_ref.at[slot],
                sems.at[slot],
            )
            for slot in range(NZ)
        ]
        for copy in copies:
            copy.start()
        for copy in copies:
            copy.wait()

    return pl.pallas_call(
        kernel,
        out_shape=pltpu.VMEM((NZ, ROWS, DEPTH), jnp.bfloat16),
        in_specs=[SMEM, ANYWHERE],
        out_specs=ANYWHERE,
        scratch_shapes=[pltpu.SemaphoreType.DMA((NZ,))],
        compiler_params=pltpu.CompilerParams(vmem_limit_bytes=4 << 20),
        cost_estimate=pl.CostEstimate(flops=0, bytes_accessed=16 << 20, transcendentals=0),
        name="hold_tokens",
    )(place, pltpu.with_memory_space_constraint(tokens, pltpu.HBM))


def project_early(place, pieces, held_sets):
    offsets = slots_of(pieces)
    count = len(offsets)

    def kernel(place_ref, *refs):
        sources, held_refs = refs[: len(pieces)], refs[len(pieces) : len(pieces) + 2]
        out_refs, (weight, sem_w) = refs[len(pieces) + 2 : len(pieces) + 4], refs[len(pieces) + 4 :]
        weights = weight_copies(place_ref, pieces, sources, weight, sem_w)
        for group in weights:
            for copy in group:
                copy.start()
        for slot, offset in enumerate(offsets):
            for copy in weights[slot]:
                copy.wait()
            for held_ref, out_ref in zip(held_refs, out_refs):
                product = jnp.dot(
                    held_ref[slot_of(offset)],
                    weight[slot * DEPTH : (slot + 1) * DEPTH],
                    preferred_element_type=jnp.float32,
                )
                if slot == 0:
                    out_ref[...] = product
                else:
                    out_ref[...] += product

    shape = pltpu.VMEM((ROWS, COLS), jnp.float32)
    return pl.pallas_call(
        kernel,
        out_shape=(shape, shape),
        in_specs=[SMEM] + [ANYWHERE] * len(pieces) + [VMEM] * 2,
        out_specs=(VMEM, VMEM),
        scratch_shapes=[
            pltpu.VMEM((count * DEPTH, COLS), jnp.bfloat16),
            pltpu.SemaphoreType.DMA((len(pieces),)),
        ],
        compiler_params=pltpu.CompilerParams(vmem_limit_bytes=16 << 20),
        cost_estimate=pl.CostEstimate(
            flops=4 * ROWS * count * DEPTH * COLS, bytes_accessed=18 << 20, transcendentals=0
        ),
        name="project_early",
    )(place, *[piece[0] for piece in pieces], *held_sets)


def project_late(place, pieces, held, partial, cosine, sine, query_gain, key_gain, ready=None):
    offsets = slots_of(pieces)
    count = len(offsets)
    n_in = len(pieces) if ready is None else 1

    def kernel(place_ref, *refs):
        sources = refs[:n_in]
        held_ref, partial_ref, cos_ref, sin_ref, qgain_ref, kgain_ref, out_ref = refs[n_in : n_in + 7]
        core = place_ref[2]
        weights = [[] for _ in offsets]
        if ready is None:
            weight, sem_w = refs[n_in + 7 :]
            weights = weight_copies(place_ref, pieces, sources, weight, sem_w)
        else:
            weight = sources[0]
        for group in weights:
            for copy in group:
                copy.start()

        def normed(field, gain, rows):
            factor = lax.rsqrt(jnp.mean(field * field, axis=1, keepdims=True) + NORM_EPS)
            field = field * factor * gain
            return field * cos_ref[rows] + pltpu.roll(field, HEAD // 2, 1) * sin_ref[rows]

        for tile in range(TILES):
            rows = pl.ds(tile * TILE, TILE)
            result = partial_ref[rows]
            for slot, offset in enumerate(offsets):
                if tile == 0:
                    for copy in weights[slot]:
                        copy.wait()
                result = result + jnp.dot(
                    held_ref[slot_of(offset), rows],
                    weight[slot * DEPTH : (slot + 1) * DEPTH],
                    preferred_element_type=jnp.float32,
                )
            raw = result[:, :HEAD]
            key = normed(raw, kgain_ref[...], rows)
            out_ref[rows, :HEAD] = jnp.where(core == 0, key, raw).astype(jnp.bfloat16)
            for first in range(HEAD, COLS, HEAD):
                field = normed(result[:, first : first + HEAD], qgain_ref[...], rows)
                out_ref[rows, first : first + HEAD] = field.astype(jnp.bfloat16)

    shape = jax.ShapeDtypeStruct((ROWS, COLS), jnp.bfloat16)
    weight_shape = pltpu.VMEM((count * DEPTH, COLS), jnp.bfloat16)
    first = ready is None
    return pl.pallas_call(
        kernel,
        out_shape=(shape, weight_shape) if first else shape,
        in_specs=[SMEM] + ([ANYWHERE] * n_in if first else [VMEM]) + [VMEM] * 6,
        out_specs=(VMEM, VMEM) if first else VMEM,
        scratch_shapes=[pltpu.SemaphoreType.DMA((len(pieces),))] if first else [],
        compiler_params=pltpu.CompilerParams(vmem_limit_bytes=16 << 20),
        cost_estimate=pl.CostEstimate(
            flops=2 * ROWS * count * DEPTH * COLS, bytes_accessed=9 << 20, transcendentals=0
        ),
        name="project_late",
    )(
        place, *([piece[0] for piece in pieces] if first else [ready]), held, partial, cosine, sine,
        query_gain, key_gain,
    )


def attend(place, own, received, request_start):
    scale = math.log2(math.e) / math.sqrt(HEAD)

    def kernel(place_ref, own_ref, received_ref, start_ref, out_ref, key_ref, value_ref):
        core = place_ref[2]
        key_ref[...] = jnp.where(core == 0, own_ref[:, :HEAD], received_ref[:, :HEAD])
        value_ref[:, :HEAD] = jnp.where(core == 0, received_ref[:, :HEAD], own_ref[:, :HEAD])
        value_ref[:, HEAD:] = jnp.ones((ROWS, HEAD), jnp.bfloat16)
        for block in range(ROWS // QBLOCK):
            rows = pl.ds(block * QBLOCK, QBLOCK)
            low = max(0, block * QBLOCK - LONGEST + 1) // QBLOCK * QBLOCK
            count = (block + 1) * QBLOCK - low
            keys, values = key_ref[pl.ds(low, count)], value_ref[pl.ds(low, count)]
            row_ids = block * QBLOCK + lax.broadcasted_iota(jnp.int32, (QBLOCK, count), 0)
            key_ids = low + lax.broadcasted_iota(jnp.int32, (QBLOCK, count), 1)
            allowed = (key_ids <= row_ids) & (key_ids >= start_ref[rows])
            bias = jnp.where(allowed, 0.0, -1e30)
            for side, source in enumerate((own_ref, received_ref)):
                first = pl.multiple_of((core if side == 0 else 1 - core) * 512, 512)
                queries = jnp.concatenate(
                    [source[rows, head * HEAD : (head + 1) * HEAD] for head in range(1, 5)], axis=0
                )
                scores = lax.dot_general(
                    queries, keys, (((1,), (1,)), ((), ())), preferred_element_type=jnp.float32
                )
                scores = scores.reshape(4, QBLOCK, count) * scale + bias[None]
                scores = scores.reshape(4 * QBLOCK, count)
                top = jnp.max(scores, axis=1, keepdims=True)
                weights = jnp.exp2(scores - top).astype(jnp.bfloat16)
                mixed = jnp.dot(weights, values, preferred_element_type=jnp.float32)
                mixed = (mixed[:, :HEAD] / mixed[:, HEAD:]).astype(jnp.bfloat16)
                for head in range(4):
                    out_ref[rows, pl.ds(first + head * HEAD, HEAD)] = mixed[
                        head * QBLOCK : (head + 1) * QBLOCK
                    ]

    return pl.pallas_call(
        kernel,
        out_shape=jax.ShapeDtypeStruct((ROWS, 8 * HEAD), jnp.bfloat16),
        in_specs=[SMEM, VMEM, VMEM, VMEM],
        out_specs=VMEM,
        scratch_shapes=[
            pltpu.VMEM((ROWS, HEAD), jnp.bfloat16),
            pltpu.VMEM((ROWS, 2 * HEAD), jnp.bfloat16),
        ],
        compiler_params=pltpu.CompilerParams(vmem_limit_bytes=32 << 20),
        cost_estimate=pl.CostEstimate(
            flops=4 * 8 * ROWS * 512 * HEAD, bytes_accessed=4 << 20, transcendentals=8 * ROWS * 512
        ),
        name="attend",
    )(place, own, received, request_start)


def shards(tokens, lengths, qkv_weight, query_norm_gain, key_norm_gain):
    place = jnp.stack([lax.axis_index("z"), lax.axis_index("xh"), lax.axis_index("c")]).astype(
        jnp.int32
    )
    other_tokens = lax.ppermute(tokens, "c", SWAP)
    other_lengths = lax.ppermute(lengths, "c", SWAP)
    spread = regroup(qkv_weight).reshape(16, -1, COLS)
    block = lax.all_to_all(spread, ("c",) + TENSOR, split_axis=0, concat_axis=0, tiled=True)
    own_start, other_start = request_starts(lengths[0]), request_starts(other_lengths[0])
    own_tables, other_tables = rotary_tables(own_start), rotary_tables(other_start)
    held = hold_tokens(place, tokens)
    other_held = hold_tokens(place, other_tokens)
    early, late, *ahead = gather_blocks(
        block.reshape(GROUP, COLS), (held, other_held, *own_tables, *other_tables)
    )
    held, other_held, *tables = ahead[0]
    own_tables, other_tables = tables[:2], tables[2:]
    gains = (query_norm_gain.reshape(1, HEAD), key_norm_gain.reshape(1, HEAD))
    own_partial, other_partial = project_early(place, early, (held, other_held))
    other, ready = project_late(place, late, other_held, other_partial, *other_tables, *gains)
    received = lax.ppermute(other, "c", SWAP)
    own = project_late(place, late, held, own_partial, *own_tables, *gains, ready)
    return attend(place, own, received, own_start.reshape(ROWS, 1))


def solution(mesh):
    fine = Mesh(mesh.devices.reshape(NZ, 2, 2, 4, 2), ("z", "xh", "c") + TENSOR)
    rows = ("z", "xh", "c")
    in_specs = (P(rows, None), P(rows, None), P(rows + TENSOR, None), P(), P())
    return jax.shard_map(
        shards, mesh=fine, in_specs=in_specs, out_specs=P(rows, TENSOR), check_vma=False
    )
```

```python
import math

import jax
import jax.numpy as jnp
from jax import lax
from jax.experimental import pallas as pl
from jax.experimental.pallas import tpu as pltpu
from jax.sharding import Mesh, PartitionSpec as P

ROPE_BASE = 1000000.0
NORM_EPS = 1e-06

HEAD = 128
HEADS = 8
ROWS = 768
NZ = 8
GROUP = 320
DEPTH = 2 * GROUP
COLS = 640
TILE = 256
TILES = ROWS // TILE
LONGEST = 384
QBLOCK = 128
TENSOR = ("y", "xl")
UP = [(z, (z + 1) % NZ) for z in range(NZ)]
DOWN = [(z, (z - 1) % NZ) for z in range(NZ)]
SWAP = [(0, 1), (1, 0)]

ANYWHERE = pl.BlockSpec(memory_space=pl.ANY)
VMEM = pl.BlockSpec(memory_space=pltpu.VMEM)
SMEM = pl.BlockSpec(memory_space=pltpu.SMEM)


def request_starts(length_row):
    ending = jnp.cumsum(length_row)
    offsets = ending - length_row
    row_ids = jnp.arange(ROWS, dtype=jnp.int32)
    reached = offsets[None, :] <= row_ids[:, None]
    return jnp.max(jnp.where(reached, offsets[None, :], 0), axis=1)


def rotary_tables(request_start):
    positions = (jnp.arange(ROWS, dtype=jnp.int32) - request_start).astype(jnp.float32)
    half = HEAD // 2
    frequency = ROPE_BASE ** (-jnp.arange(half, dtype=jnp.float32) * 2.0 / HEAD)
    angles = positions[:, None] * frequency[None, :]
    cosine, sine = jnp.cos(angles), jnp.sin(angles)
    return jnp.concatenate([cosine, cosine], axis=1), jnp.concatenate([-sine, sine], axis=1)


def regroup(weight):
    rows, groups, wide = weight.shape[0], 8, COLS - HEAD

    def kernel(weight_ref, out_ref):
        for core in range(2):
            for group in range(groups):
                index = core * groups + group
                first = (HEADS + core) * HEADS * HEAD + group * HEAD
                out_ref[index, :, :HEAD] = weight_ref[:, first : first + HEAD]
                first = (group * 2 + core) * wide
                out_ref[index, :, HEAD:] = weight_ref[:, first : first + wide]

    return pl.pallas_call(
        kernel,
        out_shape=jax.ShapeDtypeStruct((2 * groups, rows, COLS), weight.dtype),
        in_specs=[VMEM],
        out_specs=VMEM,
        compiler_params=pltpu.CompilerParams(vmem_limit_bytes=8 << 20),
        name="regroup",
    )(weight)


def gather_blocks(place, block, ahead):
    half = GROUP // 2

    def up(array):
        return lax.ppermute(array, "z", UP)

    def down(array):
        return lax.ppermute(array, "z", DOWN)

    def across(array):
        return lax.ppermute(array, "xh", SWAP)

    other = across(block)
    up1, down1 = up(block), down(block)
    up1, down1, ahead = lax.optimization_barrier((up1, down1, ahead))
    up2, down2 = up(up1), down(down1)
    up1, other = lax.optimization_barrier((up1, other))
    other_up1 = across(up1)
    other_down1 = down(other)
    up3, down3 = up(up2), down(down2)
    other_down2 = across(down2)
    other_up2 = up(other_up1)
    first = [
        (block, 0, 0, 0), (other, 0, 1, 0), (up1, -1, 0, 0), (other_up1, -1, 1, 0),
    ]
    totals = project_early(place, first, ahead[:2])
    up3, down3, totals = lax.optimization_barrier((up3, down3, totals))
    up4, down4 = up(up3[:half]), down(down3[half:])
    totals = project_early(place, [(down1, 1, 0, 0), (other_down1, 1, 1, 0)], ahead[:2], totals)
    other_up2, other_down2, totals = lax.optimization_barrier((other_up2, other_down2, totals))
    other_up3, other_down3 = up(other_up2), down(other_down2)
    other_up4, other_down4 = across(up4), across(down4)
    second = [
        (up2, -2, 0, 0), (other_up2, -2, 1, 0), (down2, 2, 0, 0), (other_down2, 2, 1, 0),
    ]
    totals = project_early(place, second, ahead[:2], totals)
    last = [
        (up3, -3, 0, 0), (other_up3, -3, 1, 0), (down3, 3, 0, 0), (other_down3, 3, 1, 0),
        (up4, 4, 0, 0), (down4, 4, 0, half), (other_up4, 4, 1, 0), (other_down4, 4, 1, half),
    ]
    return last, totals, ahead


def slots_of(pieces):
    offsets = []
    for _, offset, _, _ in pieces:
        if offset not in offsets:
            offsets.append(offset)
    return offsets


def assemble(place_ref, pieces, sources, target, wanted):
    offsets = slots_of(pieces)
    for (array, offset, flip, first), source in zip(pieces, sources):
        if offsets.index(offset) == wanted:
            side = lax.rem(place_ref[1] + flip, 2)
            row = pl.multiple_of(side * GROUP + (wanted * DEPTH + first), 16)
            target[pl.ds(row, array.shape[0])] = source[...]


def slot_of(offset):
    return (offset + NZ) % NZ


def hold_tokens(place, tokens):
    def kernel(place_ref, token_ref, out_ref, sems):
        copies = [
            pltpu.make_async_copy(
                token_ref.at[
                    :, pl.ds(pl.multiple_of(lax.rem(place_ref[0] + slot, NZ) * DEPTH, HEAD), DEPTH)
                ],
                out_ref.at[slot],
                sems.at[slot],
            )
            for slot in range(NZ)
        ]
        for copy in copies:
            copy.start()
        for copy in copies:
            copy.wait()

    return pl.pallas_call(
        kernel,
        out_shape=pltpu.VMEM((NZ, ROWS, DEPTH), jnp.bfloat16),
        in_specs=[SMEM, ANYWHERE],
        out_specs=ANYWHERE,
        scratch_shapes=[pltpu.SemaphoreType.DMA((NZ,))],
        compiler_params=pltpu.CompilerParams(vmem_limit_bytes=4 << 20),
        cost_estimate=pl.CostEstimate(flops=0, bytes_accessed=16 << 20, transcendentals=0),
        name="hold_tokens",
    )(place, pltpu.with_memory_space_constraint(tokens, pltpu.HBM))


def project_early(place, pieces, held_sets, totals=()):
    offsets = slots_of(pieces)
    count = len(offsets)

    def kernel(place_ref, *refs):
        sources, held_refs = refs[: len(pieces)], refs[len(pieces) : len(pieces) + 2]
        total_refs, out_refs, weight = refs[len(pieces) + 2 : -3], refs[-3:-1], refs[-1]
        for slot, offset in enumerate(offsets):
            assemble(place_ref, pieces, sources, weight, slot)
            for which, (held_ref, out_ref) in enumerate(zip(held_refs, out_refs)):
                product = jnp.dot(
                    held_ref[slot_of(offset)],
                    weight[slot * DEPTH : (slot + 1) * DEPTH],
                    preferred_element_type=jnp.float32,
                )
                if slot:
                    out_ref[...] += product
                elif total_refs:
                    out_ref[...] = total_refs[which][...] + product
                else:
                    out_ref[...] = product

    shape = pltpu.VMEM((ROWS, COLS), jnp.float32)
    return pl.pallas_call(
        kernel,
        out_shape=(shape, shape),
        in_specs=[SMEM] + [VMEM] * (len(pieces) + 2 + len(totals)),
        out_specs=(VMEM, VMEM),
        input_output_aliases={len(pieces) + 3 + which: which for which in range(len(totals))},
        scratch_shapes=[pltpu.VMEM((count * DEPTH, COLS), jnp.bfloat16)],
        compiler_params=pltpu.CompilerParams(vmem_limit_bytes=16 << 20),
        cost_estimate=pl.CostEstimate(
            flops=4 * ROWS * count * DEPTH * COLS, bytes_accessed=18 << 20, transcendentals=0
        ),
        name="project_early",
    )(place, *[piece[0] for piece in pieces], *held_sets, *totals)


def project_late(place, pieces, held, partial, cosine, sine, query_gain, key_gain, ready=None):
    offsets = slots_of(pieces)
    count = len(offsets)
    n_in = len(pieces) if ready is None else 1

    def kernel(place_ref, *refs):
        sources = refs[:n_in]
        held_ref, partial_ref, cos_ref, sin_ref, qgain_ref, kgain_ref, out_ref = refs[n_in : n_in + 7]
        core = place_ref[2]
        weight = refs[n_in + 7] if ready is None else sources[0]

        def normed(field, gain, rows):
            factor = lax.rsqrt(jnp.mean(field * field, axis=1, keepdims=True) + NORM_EPS)
            field = field * factor * gain
            return field * cos_ref[rows] + pltpu.roll(field, HEAD // 2, 1) * sin_ref[rows]

        for tile in range(TILES):
            rows = pl.ds(tile * TILE, TILE)
            result = partial_ref[rows]
            for slot, offset in enumerate(offsets):
                if tile == 0 and ready is None:
                    assemble(place_ref, pieces, sources, weight, slot)
                result = result + jnp.dot(
                    held_ref[slot_of(offset), rows],
                    weight[slot * DEPTH : (slot + 1) * DEPTH],
                    preferred_element_type=jnp.float32,
                )
            raw = result[:, :HEAD]
            key = normed(raw, kgain_ref[...], rows)
            out_ref[rows, :HEAD] = jnp.where(core == 0, key, raw).astype(jnp.bfloat16)
            for first in range(HEAD, COLS, HEAD):
                field = normed(result[:, first : first + HEAD], qgain_ref[...], rows)
                out_ref[rows, first : first + HEAD] = field.astype(jnp.bfloat16)

    shape = jax.ShapeDtypeStruct((ROWS, COLS), jnp.bfloat16)
    weight_shape = pltpu.VMEM((count * DEPTH, COLS), jnp.bfloat16)
    first = ready is None
    return pl.pallas_call(
        kernel,
        out_shape=(shape, weight_shape) if first else shape,
        in_specs=[SMEM] + [VMEM] * (n_in + 6),
        out_specs=(VMEM, VMEM) if first else VMEM,
        compiler_params=pltpu.CompilerParams(vmem_limit_bytes=16 << 20),
        cost_estimate=pl.CostEstimate(
            flops=2 * ROWS * count * DEPTH * COLS, bytes_accessed=9 << 20, transcendentals=0
        ),
        name="project_late",
    )(
        place, *([piece[0] for piece in pieces] if first else [ready]), held, partial, cosine, sine,
        query_gain, key_gain,
    )


def attend(place, own, received, request_start):
    scale = math.log2(math.e) / math.sqrt(HEAD)

    def kernel(place_ref, own_ref, received_ref, start_ref, out_ref, key_ref, value_ref):
        core = place_ref[2]
        key_ref[...] = jnp.where(core == 0, own_ref[:, :HEAD], received_ref[:, :HEAD])
        value_ref[:, :HEAD] = jnp.where(core == 0, received_ref[:, :HEAD], own_ref[:, :HEAD])
        value_ref[:, HEAD:] = jnp.ones((ROWS, HEAD), jnp.bfloat16)
        for block in range(ROWS // QBLOCK):
            rows = pl.ds(block * QBLOCK, QBLOCK)
            low = max(0, block * QBLOCK - LONGEST + 1) // QBLOCK * QBLOCK
            count = (block + 1) * QBLOCK - low
            keys, values = key_ref[pl.ds(low, count)], value_ref[pl.ds(low, count)]
            row_ids = block * QBLOCK + lax.broadcasted_iota(jnp.int32, (QBLOCK, count), 0)
            key_ids = low + lax.broadcasted_iota(jnp.int32, (QBLOCK, count), 1)
            allowed = (key_ids <= row_ids) & (key_ids >= start_ref[rows])
            bias = jnp.where(allowed, 0.0, -1e30)
            for side, source in enumerate((own_ref, received_ref)):
                first = pl.multiple_of((core if side == 0 else 1 - core) * 512, 512)
                queries = jnp.concatenate(
                    [source[rows, head * HEAD : (head + 1) * HEAD] for head in range(1, 5)], axis=0
                )
                scores = lax.dot_general(
                    queries, keys, (((1,), (1,)), ((), ())), preferred_element_type=jnp.float32
                )
                scores = scores.reshape(4, QBLOCK, count) * scale + bias[None]
                scores = scores.reshape(4 * QBLOCK, count)
                top = jnp.max(scores, axis=1, keepdims=True)
                weights = jnp.exp2(scores - top).astype(jnp.bfloat16)
                mixed = jnp.dot(weights, values, preferred_element_type=jnp.float32)
                mixed = (mixed[:, :HEAD] / mixed[:, HEAD:]).astype(jnp.bfloat16)
                for head in range(4):
                    out_ref[rows, pl.ds(first + head * HEAD, HEAD)] = mixed[
                        head * QBLOCK : (head + 1) * QBLOCK
                    ]

    return pl.pallas_call(
        kernel,
        out_shape=jax.ShapeDtypeStruct((ROWS, 8 * HEAD), jnp.bfloat16),
        in_specs=[SMEM, VMEM, VMEM, VMEM],
        out_specs=VMEM,
        scratch_shapes=[
            pltpu.VMEM((ROWS, HEAD), jnp.bfloat16),
            pltpu.VMEM((ROWS, 2 * HEAD), jnp.bfloat16),
        ],
        compiler_params=pltpu.CompilerParams(vmem_limit_bytes=32 << 20),
        cost_estimate=pl.CostEstimate(
            flops=4 * 8 * ROWS * 512 * HEAD, bytes_accessed=4 << 20, transcendentals=8 * ROWS * 512
        ),
        name="attend",
    )(place, own, received, request_start)


def shards(tokens, lengths, qkv_weight, query_norm_gain, key_norm_gain):
    place = jnp.stack([lax.axis_index("z"), lax.axis_index("xh"), lax.axis_index("c")]).astype(
        jnp.int32
    )
    other_tokens = lax.ppermute(tokens, "c", SWAP)
    other_lengths = lax.ppermute(lengths, "c", SWAP)
    spread = regroup(qkv_weight)
    block = lax.all_to_all(spread, ("c",) + TENSOR, split_axis=0, concat_axis=0, tiled=True)
    own_start, other_start = request_starts(lengths[0]), request_starts(other_lengths[0])
    own_tables, other_tables = rotary_tables(own_start), rotary_tables(other_start)
    held = hold_tokens(place, tokens)
    other_held = hold_tokens(place, other_tokens)
    late, totals, ahead = gather_blocks(
        place, block.reshape(GROUP, COLS), (held, other_held, *own_tables, *other_tables)
    )
    held, other_held, *tables = ahead
    own_tables, other_tables = tables[:2], tables[2:]
    gains = (query_norm_gain.reshape(1, HEAD), key_norm_gain.reshape(1, HEAD))
    own_partial, other_partial = totals
    other, ready = project_late(place, late, other_held, other_partial, *other_tables, *gains)
    received = lax.ppermute(other, "c", SWAP)
    own = project_late(place, late, held, own_partial, *own_tables, *gains, ready)
    return attend(place, own, received, own_start.reshape(ROWS, 1))


def solution(mesh):
    fine = Mesh(mesh.devices.reshape(NZ, 2, 2, 4, 2), ("z", "xh", "c") + TENSOR)
    rows = ("z", "xh", "c")
    in_specs = (P(rows, None), P(rows, None), P(rows + TENSOR, None), P(), P())
    return jax.shard_map(
        shards, mesh=fine, in_specs=in_specs, out_specs=P(rows, TENSOR), check_vma=False
    )
```

```python
import math

import jax
import jax.numpy as jnp
from jax import lax
from jax.experimental import pallas as pl
from jax.experimental.pallas import tpu as pltpu
from jax.sharding import Mesh, PartitionSpec as P

ROPE_BASE = 1000000.0
NORM_EPS = 1e-06

HEAD = 128
HEADS = 8
ROWS = 768
NZ = 8
GROUP = 320
DEPTH = 2 * GROUP
COLS = 640
TILE = 256
TILES = ROWS // TILE
LONGEST = 384
QBLOCK = 128
TENSOR = ("y", "xl")
UP = [(z * 2 + c, (z + (1 - 2 * c)) % NZ * 2 + c) for z in range(NZ) for c in range(2)]
DOWN = [(target, source) for source, target in UP]
SWAP = [(0, 1), (1, 0)]

ANYWHERE = pl.BlockSpec(memory_space=pl.ANY)
VMEM = pl.BlockSpec(memory_space=pltpu.VMEM)
SMEM = pl.BlockSpec(memory_space=pltpu.SMEM)


def request_starts(length_row):
    ending = jnp.cumsum(length_row)
    offsets = ending - length_row
    row_ids = jnp.arange(ROWS, dtype=jnp.int32)
    reached = offsets[None, :] <= row_ids[:, None]
    return jnp.max(jnp.where(reached, offsets[None, :], 0), axis=1)


def rotary_tables(request_start):
    positions = (jnp.arange(ROWS, dtype=jnp.int32) - request_start).astype(jnp.float32)
    half = HEAD // 2
    frequency = ROPE_BASE ** (-jnp.arange(half, dtype=jnp.float32) * 2.0 / HEAD)
    angles = positions[:, None] * frequency[None, :]
    cosine, sine = jnp.cos(angles), jnp.sin(angles)
    return jnp.concatenate([cosine, cosine], axis=1), jnp.concatenate([-sine, sine], axis=1)


def regroup(weight):
    rows, groups, wide = weight.shape[0], 8, COLS - HEAD

    def kernel(weight_ref, out_ref):
        for core in range(2):
            for group in range(groups):
                index = core * groups + group
                first = (HEADS + core) * HEADS * HEAD + group * HEAD
                out_ref[index, :, :HEAD] = weight_ref[:, first : first + HEAD]
                first = (group * 2 + core) * wide
                out_ref[index, :, HEAD:] = weight_ref[:, first : first + wide]

    return pl.pallas_call(
        kernel,
        out_shape=jax.ShapeDtypeStruct((2 * groups, rows, COLS), weight.dtype),
        in_specs=[VMEM],
        out_specs=VMEM,
        compiler_params=pltpu.CompilerParams(vmem_limit_bytes=8 << 20),
        name="regroup",
    )(weight)


def gather_blocks(place, block, ahead):
    def up(array):
        return lax.ppermute(array, ("z", "c"), UP)

    def down(array):
        return lax.ppermute(array, ("z", "c"), DOWN)

    def across(array):
        return lax.ppermute(array, "xh", SWAP)

    other = across(block)
    up1, down1 = up(block), down(block)
    up1, down1, ahead = lax.optimization_barrier((up1, down1, ahead))
    held = ahead[:2]
    up2, down2 = up(up1), down(down1)
    up1, other = lax.optimization_barrier((up1, other))
    other_down1 = down(other)
    other_up1 = across(up1)
    totals = project_early(place, [(block, 0, 0, 0), (other, 0, 1, 0)], held)
    up2, down2, totals = lax.optimization_barrier((up2, down2, totals))
    up3, down3 = up(up2), down(down2)
    other_down2 = across(down2)
    other_up2 = up(other_up1)
    nearest = [
        (up1, -1, 0, 0), (other_up1, -1, 1, 0), (down1, 1, 0, 0), (other_down1, 1, 1, 0),
    ]
    totals = project_early(place, nearest, held, totals)
    up3, down3, totals = lax.optimization_barrier((up3, down3, totals))
    down4 = down(down3)
    other_down3 = across(down3)
    other_up3 = up(other_up2)
    second = [
        (up2, -2, 0, 0), (other_up2, -2, 1, 0), (down2, 2, 0, 0), (other_down2, 2, 1, 0),
    ]
    totals = project_early(place, second, held, totals)
    down4, totals = lax.optimization_barrier((down4, totals))
    other_down4 = across(down4)
    third = [
        (up3, -3, 0, 0), (other_up3, -3, 1, 0), (down3, 3, 0, 0), (other_down3, 3, 1, 0),
    ]
    totals = project_early(place, third, held, totals)
    last = [(down4, 4, 0, 0), (other_down4, 4, 1, 0)]
    return last, totals, ahead


def slots_of(pieces):
    offsets = []
    for _, offset, _, _ in pieces:
        if offset not in offsets:
            offsets.append(offset)
    return offsets


def assemble(place_ref, pieces, sources, target, wanted):
    offsets = slots_of(pieces)
    for (array, offset, flip, first), source in zip(pieces, sources):
        if offsets.index(offset) == wanted:
            side = lax.rem(place_ref[1] + flip, 2)
            row = pl.multiple_of(side * GROUP + (wanted * DEPTH + first), 16)
            target[pl.ds(row, array.shape[0])] = source[...]


def slot_of(offset):
    return (offset + NZ) % NZ


def hold_tokens(place, tokens):
    def kernel(place_ref, token_ref, out_ref, sems):
        z, core = place_ref[0], place_ref[2]
        wheres = [
            lax.rem(z + jnp.where(core == 0, slot, (NZ - slot) % NZ), NZ) for slot in range(NZ)
        ]
        copies = [
            pltpu.make_async_copy(
                token_ref.at[:, pl.ds(pl.multiple_of(wheres[slot] * DEPTH, HEAD), DEPTH)],
                out_ref.at[slot],
                sems.at[slot],
            )
            for slot in range(NZ)
        ]
        for copy in copies:
            copy.start()
        for copy in copies:
            copy.wait()

    return pl.pallas_call(
        kernel,
        out_shape=pltpu.VMEM((NZ, ROWS, DEPTH), jnp.bfloat16),
        in_specs=[SMEM, ANYWHERE],
        out_specs=ANYWHERE,
        scratch_shapes=[pltpu.SemaphoreType.DMA((NZ,))],
        compiler_params=pltpu.CompilerParams(vmem_limit_bytes=4 << 20),
        cost_estimate=pl.CostEstimate(flops=0, bytes_accessed=16 << 20, transcendentals=0),
        name="hold_tokens",
    )(place, pltpu.with_memory_space_constraint(tokens, pltpu.HBM))


def project_early(place, pieces, held_sets, totals=()):
    offsets = slots_of(pieces)
    count = len(offsets)

    def kernel(place_ref, *refs):
        sources, held_refs = refs[: len(pieces)], refs[len(pieces) : len(pieces) + 2]
        total_refs, out_refs, weight = refs[len(pieces) + 2 : -3], refs[-3:-1], refs[-1]
        for slot, offset in enumerate(offsets):
            assemble(place_ref, pieces, sources, weight, slot)
            for which, (held_ref, out_ref) in enumerate(zip(held_refs, out_refs)):
                product = jnp.dot(
                    held_ref[slot_of(offset)],
                    weight[slot * DEPTH : (slot + 1) * DEPTH],
                    preferred_element_type=jnp.float32,
                )
                if slot:
                    out_ref[...] += product
                elif total_refs:
                    out_ref[...] = total_refs[which][...] + product
                else:
                    out_ref[...] = product

    shape = pltpu.VMEM((ROWS, COLS), jnp.float32)
    return pl.pallas_call(
        kernel,
        out_shape=(shape, shape),
        in_specs=[SMEM] + [VMEM] * (len(pieces) + 2 + len(totals)),
        out_specs=(VMEM, VMEM),
        input_output_aliases={len(pieces) + 3 + which: which for which in range(len(totals))},
        scratch_shapes=[pltpu.VMEM((count * DEPTH, COLS), jnp.bfloat16)],
        compiler_params=pltpu.CompilerParams(vmem_limit_bytes=16 << 20),
        cost_estimate=pl.CostEstimate(
            flops=4 * ROWS * count * DEPTH * COLS, bytes_accessed=18 << 20, transcendentals=0
        ),
        name="project_early",
    )(place, *[piece[0] for piece in pieces], *held_sets, *totals)


def project_late(place, pieces, held, partial, cosine, sine, query_gain, key_gain, ready=None):
    offsets = slots_of(pieces)
    count = len(offsets)
    n_in = len(pieces) if ready is None else 1

    def kernel(place_ref, *refs):
        sources = refs[:n_in]
        held_ref, partial_ref, cos_ref, sin_ref, qgain_ref, kgain_ref, out_ref = refs[n_in : n_in + 7]
        core = place_ref[2]
        weight = refs[n_in + 7] if ready is None else sources[0]

        def normed(field, gain, rows):
            factor = lax.rsqrt(jnp.mean(field * field, axis=1, keepdims=True) + NORM_EPS)
            field = field * factor * gain
            return field * cos_ref[rows] + pltpu.roll(field, HEAD // 2, 1) * sin_ref[rows]

        for tile in range(TILES):
            rows = pl.ds(tile * TILE, TILE)
            result = partial_ref[rows]
            for slot, offset in enumerate(offsets):
                if tile == 0 and ready is None:
                    assemble(place_ref, pieces, sources, weight, slot)
                result = result + jnp.dot(
                    held_ref[slot_of(offset), rows],
                    weight[slot * DEPTH : (slot + 1) * DEPTH],
                    preferred_element_type=jnp.float32,
                )
            raw = result[:, :HEAD]
            key = normed(raw, kgain_ref[...], rows)
            out_ref[rows, :HEAD] = jnp.where(core == 0, key, raw).astype(jnp.bfloat16)
            for first in range(HEAD, COLS, HEAD):
                field = normed(result[:, first : first + HEAD], qgain_ref[...], rows)
                out_ref[rows, first : first + HEAD] = field.astype(jnp.bfloat16)

    shape = jax.ShapeDtypeStruct((ROWS, COLS), jnp.bfloat16)
    weight_shape = pltpu.VMEM((count * DEPTH, COLS), jnp.bfloat16)
    first = ready is None
    return pl.pallas_call(
        kernel,
        out_shape=(shape, weight_shape) if first else shape,
        in_specs=[SMEM] + [VMEM] * (n_in + 6),
        out_specs=(VMEM, VMEM) if first else VMEM,
        compiler_params=pltpu.CompilerParams(vmem_limit_bytes=16 << 20),
        cost_estimate=pl.CostEstimate(
            flops=2 * ROWS * count * DEPTH * COLS, bytes_accessed=9 << 20, transcendentals=0
        ),
        name="project_late",
    )(
        place, *([piece[0] for piece in pieces] if first else [ready]), held, partial, cosine, sine,
        query_gain, key_gain,
    )


def attend(place, own, received, request_start):
    scale = math.log2(math.e) / math.sqrt(HEAD)

    def kernel(place_ref, own_ref, received_ref, start_ref, out_ref, key_ref, value_ref):
        core = place_ref[2]
        key_ref[...] = jnp.where(core == 0, own_ref[:, :HEAD], received_ref[:, :HEAD])
        value_ref[:, :HEAD] = jnp.where(core == 0, received_ref[:, :HEAD], own_ref[:, :HEAD])
        value_ref[:, HEAD:] = jnp.ones((ROWS, HEAD), jnp.bfloat16)
        for block in range(ROWS // QBLOCK):
            rows = pl.ds(block * QBLOCK, QBLOCK)
            low = max(0, block * QBLOCK - LONGEST + 1) // QBLOCK * QBLOCK
            count = (block + 1) * QBLOCK - low
            keys, values = key_ref[pl.ds(low, count)], value_ref[pl.ds(low, count)]
            row_ids = block * QBLOCK + lax.broadcasted_iota(jnp.int32, (QBLOCK, count), 0)
            key_ids = low + lax.broadcasted_iota(jnp.int32, (QBLOCK, count), 1)
            allowed = (key_ids <= row_ids) & (key_ids >= start_ref[rows])
            bias = jnp.where(allowed, 0.0, -1e30)
            for side, source in enumerate((own_ref, received_ref)):
                first = pl.multiple_of((core if side == 0 else 1 - core) * 512, 512)
                queries = jnp.concatenate(
                    [source[rows, head * HEAD : (head + 1) * HEAD] for head in range(1, 5)], axis=0
                )
                scores = lax.dot_general(
                    queries, keys, (((1,), (1,)), ((), ())), preferred_element_type=jnp.float32
                )
                scores = scores.reshape(4, QBLOCK, count) * scale + bias[None]
                scores = scores.reshape(4 * QBLOCK, count)
                top = jnp.max(scores, axis=1, keepdims=True)
                weights = jnp.exp2(scores - top).astype(jnp.bfloat16)
                mixed = jnp.dot(weights, values, preferred_element_type=jnp.float32)
                mixed = (mixed[:, :HEAD] / mixed[:, HEAD:]).astype(jnp.bfloat16)
                for head in range(4):
                    out_ref[rows, pl.ds(first + head * HEAD, HEAD)] = mixed[
                        head * QBLOCK : (head + 1) * QBLOCK
                    ]

    return pl.pallas_call(
        kernel,
        out_shape=jax.ShapeDtypeStruct((ROWS, 8 * HEAD), jnp.bfloat16),
        in_specs=[SMEM, VMEM, VMEM, VMEM],
        out_specs=VMEM,
        scratch_shapes=[
            pltpu.VMEM((ROWS, HEAD), jnp.bfloat16),
            pltpu.VMEM((ROWS, 2 * HEAD), jnp.bfloat16),
        ],
        compiler_params=pltpu.CompilerParams(vmem_limit_bytes=32 << 20),
        cost_estimate=pl.CostEstimate(
            flops=4 * 8 * ROWS * 512 * HEAD, bytes_accessed=4 << 20, transcendentals=8 * ROWS * 512
        ),
        name="attend",
    )(place, own, received, request_start)


def shards(tokens, lengths, qkv_weight, query_norm_gain, key_norm_gain):
    place = jnp.stack([lax.axis_index("z"), lax.axis_index("xh"), lax.axis_index("c")]).astype(
        jnp.int32
    )
    other_tokens = lax.ppermute(tokens, "c", SWAP)
    other_lengths = lax.ppermute(lengths, "c", SWAP)
    spread = regroup(qkv_weight)
    block = lax.all_to_all(spread, ("c",) + TENSOR, split_axis=0, concat_axis=0, tiled=True)
    own_start, other_start = request_starts(lengths[0]), request_starts(other_lengths[0])
    own_tables, other_tables = rotary_tables(own_start), rotary_tables(other_start)
    held = hold_tokens(place, tokens)
    other_held = hold_tokens(place, other_tokens)
    late, totals, ahead = gather_blocks(
        place, block.reshape(GROUP, COLS), (held, other_held, *own_tables, *other_tables)
    )
    held, other_held, *tables = ahead
    own_tables, other_tables = tables[:2], tables[2:]
    gains = (query_norm_gain.reshape(1, HEAD), key_norm_gain.reshape(1, HEAD))
    own_partial, other_partial = totals
    other, ready = project_late(place, late, other_held, other_partial, *other_tables, *gains)
    received = lax.ppermute(other, "c", SWAP)
    own = project_late(place, late, held, own_partial, *own_tables, *gains, ready)
    return attend(place, own, received, own_start.reshape(ROWS, 1))


def solution(mesh):
    fine = Mesh(mesh.devices.reshape(NZ, 2, 2, 4, 2), ("z", "xh", "c") + TENSOR)
    rows = ("z", "xh", "c")
    in_specs = (P(rows, None), P(rows, None), P(rows + TENSOR, None), P(), P())
    return jax.shard_map(
        shards, mesh=fine, in_specs=in_specs, out_specs=P(rows, TENSOR), check_vma=False
    )
```

```python
import math

import jax
import jax.numpy as jnp
from jax import lax
from jax.experimental import pallas as pl
from jax.experimental.pallas import tpu as pltpu
from jax.sharding import Mesh, PartitionSpec as P

ROPE_BASE = 1000000.0
NORM_EPS = 1e-06

HEAD = 128
HEADS = 8
ROWS = 768
NZ = 8
GROUP = 320
DEPTH = 2 * GROUP
COLS = 640
TILE = 256
TILES = ROWS // TILE
LONGEST = 384
QBLOCK = 128
TENSOR = ("y", "xl")
UP = [(z * 2 + c, (z + (1 - 2 * c)) % NZ * 2 + c) for z in range(NZ) for c in range(2)]
DOWN = [(target, source) for source, target in UP]
SWAP = [(0, 1), (1, 0)]

ANYWHERE = pl.BlockSpec(memory_space=pl.ANY)
VMEM = pl.BlockSpec(memory_space=pltpu.VMEM)
SMEM = pl.BlockSpec(memory_space=pltpu.SMEM)


def request_starts(length_row):
    ending = jnp.cumsum(length_row)
    offsets = ending - length_row
    row_ids = jnp.arange(ROWS, dtype=jnp.int32)
    reached = offsets[None, :] <= row_ids[:, None]
    return jnp.max(jnp.where(reached, offsets[None, :], 0), axis=1)


def rotary_tables(request_start):
    positions = (jnp.arange(ROWS, dtype=jnp.int32) - request_start).astype(jnp.float32)
    half = HEAD // 2
    frequency = ROPE_BASE ** (-jnp.arange(half, dtype=jnp.float32) * 2.0 / HEAD)
    angles = positions[:, None] * frequency[None, :]
    cosine, sine = jnp.cos(angles), jnp.sin(angles)
    return jnp.concatenate([cosine, cosine], axis=1), jnp.concatenate([-sine, sine], axis=1)


def regroup(weight):
    rows, groups, wide = weight.shape[0], 8, COLS - HEAD

    def kernel(weight_ref, out_ref):
        for core in range(2):
            for group in range(groups):
                index = core * groups + group
                first = (HEADS + core) * HEADS * HEAD + group * HEAD
                out_ref[index, :, :HEAD] = weight_ref[:, first : first + HEAD]
                first = (group * 2 + core) * wide
                out_ref[index, :, HEAD:] = weight_ref[:, first : first + wide]

    return pl.pallas_call(
        kernel,
        out_shape=jax.ShapeDtypeStruct((2 * groups, rows, COLS), weight.dtype),
        in_specs=[VMEM],
        out_specs=VMEM,
        compiler_params=pltpu.CompilerParams(vmem_limit_bytes=8 << 20),
        name="regroup",
    )(weight)


def gather_blocks(place, block, ahead):
    def up(array):
        return lax.ppermute(array, ("z", "c"), UP)

    def down(array):
        return lax.ppermute(array, ("z", "c"), DOWN)

    def across(array):
        return lax.ppermute(array, "xh", SWAP)

    other = across(block)
    up1, down1 = up(block), down(block)
    up1, down1, ahead = lax.optimization_barrier((up1, down1, ahead))
    held = ahead[:2]
    up2, down2 = up(up1), down(down1)
    up1, other = lax.optimization_barrier((up1, other))
    other_down1 = down(other)
    other_up1 = across(up1)
    totals = project_early(place, [(block, 0, 0, 0), (other, 0, 1, 0)], held)
    up2, down2, totals = lax.optimization_barrier((up2, down2, totals))
    up3, down3 = up(up2), down(down2)
    other_down2 = across(down2)
    other_up2 = up(other_up1)
    nearest = [
        (up1, -1, 0, 0), (other_up1, -1, 1, 0), (down1, 1, 0, 0), (other_down1, 1, 1, 0),
    ]
    totals = project_early(place, nearest, held, totals)
    up3, down3, totals = lax.optimization_barrier((up3, down3, totals))
    down4 = down(down3)
    other_down3 = across(down3)
    other_up3 = up(other_up2)
    second = [
        (up2, -2, 0, 0), (other_up2, -2, 1, 0), (down2, 2, 0, 0), (other_down2, 2, 1, 0),
    ]
    totals = project_early(place, second, held, totals)
    other_down3, totals = lax.optimization_barrier((other_down3, totals))
    other_down4 = down(other_down3)
    third = [
        (up3, -3, 0, 0), (other_up3, -3, 1, 0), (down3, 3, 0, 0), (other_down3, 3, 1, 0),
    ]
    totals = project_early(place, third, held, totals)
    last = [(down4, 4, 0, 0), (other_down4, 4, 1, 0)]
    return last, totals, ahead


def slots_of(pieces):
    offsets = []
    for _, offset, _, _ in pieces:
        if offset not in offsets:
            offsets.append(offset)
    return offsets


def assemble(place_ref, pieces, sources, target, wanted):
    offsets = slots_of(pieces)
    for (array, offset, flip, first), source in zip(pieces, sources):
        if offsets.index(offset) == wanted:
            side = lax.rem(place_ref[1] + flip, 2)
            row = pl.multiple_of(side * GROUP + (wanted * DEPTH + first), 16)
            target[pl.ds(row, array.shape[0])] = source[...]


def slot_of(offset):
    return (offset + NZ) % NZ


def hold_tokens(place, tokens):
    def kernel(place_ref, token_ref, out_ref, sems):
        z, core = place_ref[0], place_ref[2]
        wheres = [
            lax.rem(z + jnp.where(core == 0, slot, (NZ - slot) % NZ), NZ) for slot in range(NZ)
        ]
        copies = [
            pltpu.make_async_copy(
                token_ref.at[:, pl.ds(pl.multiple_of(wheres[slot] * DEPTH, HEAD), DEPTH)],
                out_ref.at[slot],
                sems.at[slot],
            )
            for slot in range(NZ)
        ]
        for copy in copies:
            copy.start()
        for copy in copies:
            copy.wait()

    return pl.pallas_call(
        kernel,
        out_shape=pltpu.VMEM((NZ, ROWS, DEPTH), jnp.bfloat16),
        in_specs=[SMEM, ANYWHERE],
        out_specs=ANYWHERE,
        scratch_shapes=[pltpu.SemaphoreType.DMA((NZ,))],
        compiler_params=pltpu.CompilerParams(vmem_limit_bytes=4 << 20),
        cost_estimate=pl.CostEstimate(flops=0, bytes_accessed=16 << 20, transcendentals=0),
        name="hold_tokens",
    )(place, pltpu.with_memory_space_constraint(tokens, pltpu.HBM))


def project_early(place, pieces, held_sets, totals=()):
    offsets = slots_of(pieces)
    count = len(offsets)

    def kernel(place_ref, *refs):
        sources, held_refs = refs[: len(pieces)], refs[len(pieces) : len(pieces) + 2]
        total_refs, out_refs, weight = refs[len(pieces) + 2 : -3], refs[-3:-1], refs[-1]
        for slot in range(count):
            assemble(place_ref, pieces, sources, weight, slot)
        for which, (held_ref, out_ref) in enumerate(zip(held_refs, out_refs)):
            for tile in range(TILES):
                rows = pl.ds(tile * TILE, TILE)
                part = jnp.concatenate(
                    [held_ref[slot_of(offset), rows] for offset in offsets], axis=1
                )
                product = jnp.dot(part, weight[...], preferred_element_type=jnp.float32)
                out_ref[rows] = total_refs[which][rows] + product if total_refs else product

    shape = pltpu.VMEM((ROWS, COLS), jnp.float32)
    return pl.pallas_call(
        kernel,
        out_shape=(shape, shape),
        in_specs=[SMEM] + [VMEM] * (len(pieces) + 2 + len(totals)),
        out_specs=(VMEM, VMEM),
        input_output_aliases={len(pieces) + 3 + which: which for which in range(len(totals))},
        scratch_shapes=[pltpu.VMEM((count * DEPTH, COLS), jnp.bfloat16)],
        compiler_params=pltpu.CompilerParams(vmem_limit_bytes=16 << 20),
        cost_estimate=pl.CostEstimate(
            flops=4 * ROWS * count * DEPTH * COLS, bytes_accessed=18 << 20, transcendentals=0
        ),
        name="project_early",
    )(place, *[piece[0] for piece in pieces], *held_sets, *totals)


def project_late(place, pieces, held, partial, cosine, sine, query_gain, key_gain, ready=None):
    offsets = slots_of(pieces)
    count = len(offsets)
    n_in = len(pieces) if ready is None else 1

    def kernel(place_ref, *refs):
        sources = refs[:n_in]
        held_ref, partial_ref, cos_ref, sin_ref, qgain_ref, kgain_ref, out_ref = refs[n_in : n_in + 7]
        core = place_ref[2]
        weight = refs[n_in + 7] if ready is None else sources[0]

        def normed(field, gain, rows):
            factor = lax.rsqrt(jnp.mean(field * field, axis=1, keepdims=True) + NORM_EPS)
            field = field * factor * gain
            return field * cos_ref[rows] + pltpu.roll(field, HEAD // 2, 1) * sin_ref[rows]

        for tile in range(TILES):
            rows = pl.ds(tile * TILE, TILE)
            result = partial_ref[rows]
            for slot, offset in enumerate(offsets):
                if tile == 0 and ready is None:
                    assemble(place_ref, pieces, sources, weight, slot)
                result = result + jnp.dot(
                    held_ref[slot_of(offset), rows],
                    weight[slot * DEPTH : (slot + 1) * DEPTH],
                    preferred_element_type=jnp.float32,
                )
            raw = result[:, :HEAD]
            key = normed(raw, kgain_ref[...], rows)
            out_ref[rows, :HEAD] = jnp.where(core == 0, key, raw).astype(jnp.bfloat16)
            for first in range(HEAD, COLS, HEAD):
                field = normed(result[:, first : first + HEAD], qgain_ref[...], rows)
                out_ref[rows, first : first + HEAD] = field.astype(jnp.bfloat16)

    shape = jax.ShapeDtypeStruct((ROWS, COLS), jnp.bfloat16)
    weight_shape = pltpu.VMEM((count * DEPTH, COLS), jnp.bfloat16)
    first = ready is None
    return pl.pallas_call(
        kernel,
        out_shape=(shape, weight_shape) if first else shape,
        in_specs=[SMEM] + [VMEM] * (n_in + 6),
        out_specs=(VMEM, VMEM) if first else VMEM,
        compiler_params=pltpu.CompilerParams(vmem_limit_bytes=16 << 20),
        cost_estimate=pl.CostEstimate(
            flops=2 * ROWS * count * DEPTH * COLS, bytes_accessed=9 << 20, transcendentals=0
        ),
        name="project_late",
    )(
        place, *([piece[0] for piece in pieces] if first else [ready]), held, partial, cosine, sine,
        query_gain, key_gain,
    )


def attend(place, own, received, request_start):
    scale = math.log2(math.e) / math.sqrt(HEAD)

    def kernel(place_ref, own_ref, received_ref, start_ref, out_hbm, key_ref, value_ref, out_ref, sems):
        core = place_ref[2]

        def written(block):
            rows = pl.ds(block * QBLOCK, QBLOCK)
            return pltpu.make_async_copy(out_ref.at[rows], out_hbm.at[rows], sems.at[block])

        key_ref[...] = jnp.where(core == 0, own_ref[:, :HEAD], received_ref[:, :HEAD])
        value_ref[:, :HEAD] = jnp.where(core == 0, received_ref[:, :HEAD], own_ref[:, :HEAD])
        value_ref[:, HEAD:] = jnp.ones((ROWS, HEAD), jnp.bfloat16)
        for block in range(ROWS // QBLOCK):
            rows = pl.ds(block * QBLOCK, QBLOCK)
            low = max(0, block * QBLOCK - LONGEST + 1) // QBLOCK * QBLOCK
            count = (block + 1) * QBLOCK - low
            keys, values = key_ref[pl.ds(low, count)], value_ref[pl.ds(low, count)]
            row_ids = block * QBLOCK + lax.broadcasted_iota(jnp.int32, (QBLOCK, count), 0)
            key_ids = low + lax.broadcasted_iota(jnp.int32, (QBLOCK, count), 1)
            allowed = (key_ids <= row_ids) & (key_ids >= start_ref[rows])
            bias = jnp.where(allowed, 0.0, -1e30)
            for side, source in enumerate((own_ref, received_ref)):
                first = pl.multiple_of((core if side == 0 else 1 - core) * 512, 512)
                queries = jnp.concatenate(
                    [source[rows, head * HEAD : (head + 1) * HEAD] for head in range(1, 5)], axis=0
                )
                scores = lax.dot_general(
                    queries, keys, (((1,), (1,)), ((), ())), preferred_element_type=jnp.float32
                )
                scores = scores.reshape(4, QBLOCK, count) * scale + bias[None]
                scores = scores.reshape(4 * QBLOCK, count)
                top = jnp.max(scores, axis=1, keepdims=True)
                weights = jnp.exp2(scores - top).astype(jnp.bfloat16)
                mixed = jnp.dot(weights, values, preferred_element_type=jnp.float32)
                mixed = (mixed[:, :HEAD] / mixed[:, HEAD:]).astype(jnp.bfloat16)
                for head in range(4):
                    out_ref[rows, pl.ds(first + head * HEAD, HEAD)] = mixed[
                        head * QBLOCK : (head + 1) * QBLOCK
                    ]
            written(block).start()
        for block in range(ROWS // QBLOCK):
            written(block).wait()

    return pl.pallas_call(
        kernel,
        out_shape=jax.ShapeDtypeStruct((ROWS, 8 * HEAD), jnp.bfloat16),
        in_specs=[SMEM, VMEM, VMEM, VMEM],
        out_specs=ANYWHERE,
        scratch_shapes=[
            pltpu.VMEM((ROWS, HEAD), jnp.bfloat16),
            pltpu.VMEM((ROWS, 2 * HEAD), jnp.bfloat16),
            pltpu.VMEM((ROWS, HEADS * HEAD), jnp.bfloat16),
            pltpu.SemaphoreType.DMA((ROWS // QBLOCK,)),
        ],
        compiler_params=pltpu.CompilerParams(vmem_limit_bytes=32 << 20),
        cost_estimate=pl.CostEstimate(
            flops=4 * 8 * ROWS * 512 * HEAD, bytes_accessed=4 << 20, transcendentals=8 * ROWS * 512
        ),
        name="attend",
    )(place, own, received, request_start)


def shards(tokens, lengths, qkv_weight, query_norm_gain, key_norm_gain):
    place = jnp.stack([lax.axis_index("z"), lax.axis_index("xh"), lax.axis_index("c")]).astype(
        jnp.int32
    )
    other_tokens = lax.ppermute(tokens, "c", SWAP)
    other_lengths = lax.ppermute(lengths, "c", SWAP)
    spread = regroup(qkv_weight)
    block = lax.all_to_all(spread, ("c",) + TENSOR, split_axis=0, concat_axis=0, tiled=True)
    own_start, other_start = request_starts(lengths[0]), request_starts(other_lengths[0])
    own_tables, other_tables = rotary_tables(own_start), rotary_tables(other_start)
    block, own_tables, other_tables = lax.optimization_barrier((block, own_tables, other_tables))
    held = hold_tokens(place, tokens)
    other_held = hold_tokens(place, other_tokens)
    late, totals, ahead = gather_blocks(
        place, block.reshape(GROUP, COLS), (held, other_held, *own_tables, *other_tables)
    )
    held, other_held, *tables = ahead
    own_tables, other_tables = tables[:2], tables[2:]
    gains = (query_norm_gain.reshape(1, HEAD), key_norm_gain.reshape(1, HEAD))
    own_partial, other_partial = totals
    other, ready = project_late(place, late, other_held, other_partial, *other_tables, *gains)
    received = lax.ppermute(other, "c", SWAP)
    own = project_late(place, late, held, own_partial, *own_tables, *gains, ready)
    return attend(place, own, received, own_start.reshape(ROWS, 1))


def solution(mesh):
    fine = Mesh(mesh.devices.reshape(NZ, 2, 2, 4, 2), ("z", "xh", "c") + TENSOR)
    rows = ("z", "xh", "c")
    in_specs = (P(rows, None), P(rows, None), P(rows + TENSOR, None), P(), P())
    return jax.shard_map(
        shards, mesh=fine, in_specs=in_specs, out_specs=P(rows, TENSOR), check_vma=False
    )
```

```python
import math

import jax
import jax.numpy as jnp
from jax import lax
from jax.experimental import pallas as pl
from jax.experimental.pallas import tpu as pltpu
from jax.sharding import Mesh, PartitionSpec as P

ROPE_BASE = 1000000.0
NORM_EPS = 1e-06

HEAD = 128
HEADS = 8
ROWS = 768
NZ = 8
GROUP = 320
DEPTH = 2 * GROUP
COLS = 640
TILE = 256
TILES = ROWS // TILE
LONGEST = 384
QBLOCK = 128
TENSOR = ("y", "xl")
UP = [(z * 2 + c, (z + (1 - 2 * c)) % NZ * 2 + c) for z in range(NZ) for c in range(2)]
DOWN = [(target, source) for source, target in UP]
SWAP = [(0, 1), (1, 0)]

ANYWHERE = pl.BlockSpec(memory_space=pl.ANY)
VMEM = pl.BlockSpec(memory_space=pltpu.VMEM)
SMEM = pl.BlockSpec(memory_space=pltpu.SMEM)


def request_starts(length_row):
    ending = jnp.cumsum(length_row)
    offsets = ending - length_row
    row_ids = jnp.arange(ROWS, dtype=jnp.int32)
    reached = offsets[None, :] <= row_ids[:, None]
    return jnp.max(jnp.where(reached, offsets[None, :], 0), axis=1)


def rotary_tables(request_start):
    positions = (jnp.arange(ROWS, dtype=jnp.int32) - request_start).astype(jnp.float32)
    half = HEAD // 2
    frequency = ROPE_BASE ** (-jnp.arange(half, dtype=jnp.float32) * 2.0 / HEAD)
    angles = positions[:, None] * frequency[None, :]
    cosine, sine = jnp.cos(angles), jnp.sin(angles)
    return jnp.concatenate([cosine, cosine], axis=1), jnp.concatenate([-sine, sine], axis=1)


def regroup(weight):
    rows, groups, wide = weight.shape[0], 8, COLS - HEAD

    def kernel(weight_ref, out_ref):
        for core in range(2):
            for group in range(groups):
                index = core * groups + group
                first = (HEADS + core) * HEADS * HEAD + group * HEAD
                out_ref[index, :, :HEAD] = weight_ref[:, first : first + HEAD]
                first = (group * 2 + core) * wide
                out_ref[index, :, HEAD:] = weight_ref[:, first : first + wide]

    return pl.pallas_call(
        kernel,
        out_shape=jax.ShapeDtypeStruct((2 * groups, rows, COLS), weight.dtype),
        in_specs=[VMEM],
        out_specs=VMEM,
        compiler_params=pltpu.CompilerParams(vmem_limit_bytes=8 << 20),
        name="regroup",
    )(weight)


def gather_blocks(place, block, ahead):
    def up(array):
        return lax.ppermute(array, ("z", "c"), UP)

    def down(array):
        return lax.ppermute(array, ("z", "c"), DOWN)

    def across(array):
        return lax.ppermute(array, "xh", SWAP)

    other = across(block)
    up1, down1 = up(block), down(block)
    up1, down1, ahead = lax.optimization_barrier((up1, down1, ahead))
    held = ahead[:2]
    up2, down2 = up(up1), down(down1)
    up1, other = lax.optimization_barrier((up1, other))
    other_down1 = down(other)
    other_up1 = across(up1)
    totals = project_early(place, [(block, 0, 0, 0), (other, 0, 1, 0)], held)
    up2, down2, totals = lax.optimization_barrier((up2, down2, totals))
    up3, down3 = up(up2), down(down2)
    other_down2 = across(down2)
    other_up2 = up(other_up1)
    nearest = [
        (up1, -1, 0, 0), (other_up1, -1, 1, 0), (down1, 1, 0, 0), (other_down1, 1, 1, 0),
    ]
    totals = project_early(place, nearest, held, totals)
    up3, down3, totals = lax.optimization_barrier((up3, down3, totals))
    down4 = down(down3)
    other_down3 = across(down3)
    other_up3 = up(other_up2)
    second = [
        (up2, -2, 0, 0), (other_up2, -2, 1, 0), (down2, 2, 0, 0), (other_down2, 2, 1, 0),
    ]
    totals = project_early(place, second, held, totals)
    other_down3, totals = lax.optimization_barrier((other_down3, totals))
    other_down4 = down(other_down3)
    third = [
        (up3, -3, 0, 0), (other_up3, -3, 1, 0), (down3, 3, 0, 0), (other_down3, 3, 1, 0),
    ]
    totals = project_early(place, third, held, totals)
    last = [(down4, 4, 0, 0), (other_down4, 4, 1, 0)]
    return last, totals, ahead


def slots_of(pieces):
    offsets = []
    for _, offset, _, _ in pieces:
        if offset not in offsets:
            offsets.append(offset)
    return offsets


def assemble(place_ref, pieces, sources, target, wanted):
    offsets = slots_of(pieces)
    for (array, offset, flip, first), source in zip(pieces, sources):
        if offsets.index(offset) == wanted:
            side = lax.rem(place_ref[1] + flip, 2)
            row = pl.multiple_of(side * GROUP + (wanted * DEPTH + first), 16)
            target[pl.ds(row, array.shape[0])] = source[...]


def slot_of(offset):
    return (offset + NZ) % NZ


def hold_tokens(place, tokens):
    def kernel(place_ref, token_ref, out_ref, sems):
        z, core = place_ref[0], place_ref[2]
        wheres = [
            lax.rem(z + jnp.where(core == 0, slot, (NZ - slot) % NZ), NZ) for slot in range(NZ)
        ]
        copies = [
            pltpu.make_async_copy(
                token_ref.at[:, pl.ds(pl.multiple_of(wheres[slot] * DEPTH, HEAD), DEPTH)],
                out_ref.at[slot],
                sems.at[slot],
            )
            for slot in range(NZ)
        ]
        for copy in copies:
            copy.start()
        for copy in copies:
            copy.wait()

    return pl.pallas_call(
        kernel,
        out_shape=pltpu.VMEM((NZ, ROWS, DEPTH), jnp.bfloat16),
        in_specs=[SMEM, ANYWHERE],
        out_specs=ANYWHERE,
        scratch_shapes=[pltpu.SemaphoreType.DMA((NZ,))],
        compiler_params=pltpu.CompilerParams(vmem_limit_bytes=4 << 20),
        cost_estimate=pl.CostEstimate(flops=0, bytes_accessed=16 << 20, transcendentals=0),
        name="hold_tokens",
    )(place, pltpu.with_memory_space_constraint(tokens, pltpu.HBM))


def project_early(place, pieces, held_sets, totals=()):
    offsets = slots_of(pieces)
    count = len(offsets)

    def kernel(place_ref, *refs):
        sources, held_refs = refs[: len(pieces)], refs[len(pieces) : len(pieces) + 2]
        total_refs, out_refs, weight = refs[len(pieces) + 2 : -3], refs[-3:-1], refs[-1]
        for slot in range(count):
            assemble(place_ref, pieces, sources, weight, slot)
        for which, (held_ref, out_ref) in enumerate(zip(held_refs, out_refs)):
            for tile in range(TILES):
                rows = pl.ds(tile * TILE, TILE)
                part = jnp.concatenate(
                    [held_ref[slot_of(offset), rows] for offset in offsets], axis=1
                )
                product = jnp.dot(part, weight[...], preferred_element_type=jnp.float32)
                out_ref[rows] = total_refs[which][rows] + product if total_refs else product

    shape = pltpu.VMEM((ROWS, COLS), jnp.float32)
    return pl.pallas_call(
        kernel,
        out_shape=(shape, shape),
        in_specs=[SMEM] + [VMEM] * (len(pieces) + 2 + len(totals)),
        out_specs=(VMEM, VMEM),
        input_output_aliases={len(pieces) + 3 + which: which for which in range(len(totals))},
        scratch_shapes=[pltpu.VMEM((count * DEPTH, COLS), jnp.bfloat16)],
        compiler_params=pltpu.CompilerParams(vmem_limit_bytes=16 << 20),
        cost_estimate=pl.CostEstimate(
            flops=4 * ROWS * count * DEPTH * COLS, bytes_accessed=18 << 20, transcendentals=0
        ),
        name="project_early",
    )(place, *[piece[0] for piece in pieces], *held_sets, *totals)


def project_late(place, pieces, held, partial, cosine, sine, query_gain, key_gain, ready=None):
    offsets = slots_of(pieces)
    count = len(offsets)
    n_in = len(pieces) if ready is None else 1

    def kernel(place_ref, *refs):
        sources = refs[:n_in]
        held_ref, partial_ref, cos_ref, sin_ref, qgain_ref, kgain_ref, out_ref = refs[n_in : n_in + 7]
        core = place_ref[2]
        weight = refs[n_in + 7] if ready is None else sources[0]

        def normed(field, gain, rows):
            square = field * field
            upper = square.astype(jnp.bfloat16)
            lower = (square - upper.astype(jnp.float32)).astype(jnp.bfloat16)
            ones = jnp.ones((2 * HEAD, HEAD), jnp.bfloat16)
            total = jnp.dot(
                jnp.concatenate([upper, lower], axis=1), ones, preferred_element_type=jnp.float32
            )
            factor = lax.rsqrt(total * (1.0 / HEAD) + NORM_EPS)
            field = field * factor * gain
            return field * cos_ref[rows] + pltpu.roll(field, HEAD // 2, 1) * sin_ref[rows]

        for tile in range(TILES):
            rows = pl.ds(tile * TILE, TILE)
            result = partial_ref[rows]
            for slot, offset in enumerate(offsets):
                if tile == 0 and ready is None:
                    assemble(place_ref, pieces, sources, weight, slot)
                result = result + jnp.dot(
                    held_ref[slot_of(offset), rows],
                    weight[slot * DEPTH : (slot + 1) * DEPTH],
                    preferred_element_type=jnp.float32,
                )
            raw = result[:, :HEAD]
            key = normed(raw, kgain_ref[...], rows)
            out_ref[rows, :HEAD] = jnp.where(core == 0, key, raw).astype(jnp.bfloat16)
            for first in range(HEAD, COLS, HEAD):
                field = normed(result[:, first : first + HEAD], qgain_ref[...], rows)
                out_ref[rows, first : first + HEAD] = field.astype(jnp.bfloat16)

    shape = jax.ShapeDtypeStruct((ROWS, COLS), jnp.bfloat16)
    weight_shape = pltpu.VMEM((count * DEPTH, COLS), jnp.bfloat16)
    first = ready is None
    return pl.pallas_call(
        kernel,
        out_shape=(shape, weight_shape) if first else shape,
        in_specs=[SMEM] + [VMEM] * (n_in + 6),
        out_specs=(VMEM, VMEM) if first else VMEM,
        compiler_params=pltpu.CompilerParams(vmem_limit_bytes=16 << 20),
        cost_estimate=pl.CostEstimate(
            flops=2 * ROWS * count * DEPTH * COLS, bytes_accessed=9 << 20, transcendentals=0
        ),
        name="project_late",
    )(
        place, *([piece[0] for piece in pieces] if first else [ready]), held, partial, cosine, sine,
        query_gain, key_gain,
    )


def attend(place, own, received, request_start):
    scale = math.log2(math.e) / math.sqrt(HEAD)

    def kernel(place_ref, own_ref, received_ref, start_ref, out_hbm, key_ref, value_ref, out_ref, sems):
        core = place_ref[2]

        def written(block):
            rows = pl.ds(block * QBLOCK, QBLOCK)
            return pltpu.make_async_copy(out_ref.at[rows], out_hbm.at[rows], sems.at[block])

        key_ref[...] = jnp.where(core == 0, own_ref[:, :HEAD], received_ref[:, :HEAD])
        value_ref[:, :HEAD] = jnp.where(core == 0, received_ref[:, :HEAD], own_ref[:, :HEAD])
        value_ref[:, HEAD:] = jnp.ones((ROWS, HEAD), jnp.bfloat16)
        for block in range(ROWS // QBLOCK):
            rows = pl.ds(block * QBLOCK, QBLOCK)
            low = max(0, block * QBLOCK - LONGEST + 1) // QBLOCK * QBLOCK
            count = (block + 1) * QBLOCK - low
            keys, values = key_ref[pl.ds(low, count)], value_ref[pl.ds(low, count)]
            row_ids = block * QBLOCK + lax.broadcasted_iota(jnp.int32, (QBLOCK, count), 0)
            key_ids = low + lax.broadcasted_iota(jnp.int32, (QBLOCK, count), 1)
            allowed = (key_ids <= row_ids) & (key_ids >= start_ref[rows])
            bias = jnp.where(allowed, 0.0, -1e30)
            for side, source in enumerate((own_ref, received_ref)):
                first = pl.multiple_of((core if side == 0 else 1 - core) * 512, 512)
                queries = jnp.concatenate(
                    [source[rows, head * HEAD : (head + 1) * HEAD] for head in range(1, 5)], axis=0
                )
                scores = lax.dot_general(
                    queries, keys, (((1,), (1,)), ((), ())), preferred_element_type=jnp.float32
                )
                scores = (scores.reshape(4, QBLOCK, count) + bias[None]).reshape(4 * QBLOCK, count)
                top = jnp.max(scores, axis=1, keepdims=True)
                weights = jnp.exp2((scores - top) * scale).astype(jnp.bfloat16)
                mixed = jnp.dot(weights, values, preferred_element_type=jnp.float32)
                mixed = (mixed[:, :HEAD] / mixed[:, HEAD:]).astype(jnp.bfloat16)
                for head in range(4):
                    out_ref[rows, pl.ds(first + head * HEAD, HEAD)] = mixed[
                        head * QBLOCK : (head + 1) * QBLOCK
                    ]
            written(block).start()
        for block in range(ROWS // QBLOCK):
            written(block).wait()

    return pl.pallas_call(
        kernel,
        out_shape=jax.ShapeDtypeStruct((ROWS, 8 * HEAD), jnp.bfloat16),
        in_specs=[SMEM, VMEM, VMEM, VMEM],
        out_specs=ANYWHERE,
        scratch_shapes=[
            pltpu.VMEM((ROWS, HEAD), jnp.bfloat16),
            pltpu.VMEM((ROWS, 2 * HEAD), jnp.bfloat16),
            pltpu.VMEM((ROWS, HEADS * HEAD), jnp.bfloat16),
            pltpu.SemaphoreType.DMA((ROWS // QBLOCK,)),
        ],
        compiler_params=pltpu.CompilerParams(vmem_limit_bytes=32 << 20),
        cost_estimate=pl.CostEstimate(
            flops=4 * 8 * ROWS * 512 * HEAD, bytes_accessed=4 << 20, transcendentals=8 * ROWS * 512
        ),
        name="attend",
    )(place, own, received, request_start)


def shards(tokens, lengths, qkv_weight, query_norm_gain, key_norm_gain):
    place = jnp.stack([lax.axis_index("z"), lax.axis_index("xh"), lax.axis_index("c")]).astype(
        jnp.int32
    )
    other_tokens = lax.ppermute(tokens, "c", SWAP)
    other_lengths = lax.ppermute(lengths, "c", SWAP)
    spread = regroup(qkv_weight)
    block = lax.all_to_all(spread, ("c",) + TENSOR, split_axis=0, concat_axis=0, tiled=True)
    own_start, other_start = request_starts(lengths[0]), request_starts(other_lengths[0])
    own_tables, other_tables = rotary_tables(own_start), rotary_tables(other_start)
    block, own_tables, other_tables = lax.optimization_barrier((block, own_tables, other_tables))
    held = hold_tokens(place, tokens)
    other_held = hold_tokens(place, other_tokens)
    late, totals, ahead = gather_blocks(
        place, block.reshape(GROUP, COLS), (held, other_held, *own_tables, *other_tables)
    )
    held, other_held, *tables = ahead
    own_tables, other_tables = tables[:2], tables[2:]
    gains = (query_norm_gain.reshape(1, HEAD), key_norm_gain.reshape(1, HEAD))
    own_partial, other_partial = totals
    other, ready = project_late(place, late, other_held, other_partial, *other_tables, *gains)
    received = lax.ppermute(other, "c", SWAP)
    own = project_late(place, late, held, own_partial, *own_tables, *gains, ready)
    return attend(place, own, received, own_start.reshape(ROWS, 1))


def solution(mesh):
    fine = Mesh(mesh.devices.reshape(NZ, 2, 2, 4, 2), ("z", "xh", "c") + TENSOR)
    rows = ("z", "xh", "c")
    in_specs = (P(rows, None), P(rows, None), P(rows + TENSOR, None), P(), P())
    return jax.shard_map(
        shards, mesh=fine, in_specs=in_specs, out_specs=P(rows, TENSOR), check_vma=False
    )
```

```python
import math

import jax
import jax.numpy as jnp
from jax import lax
from jax.experimental import pallas as pl
from jax.experimental.pallas import tpu as pltpu
from jax.sharding import Mesh, PartitionSpec as P

ROPE_BASE = 1000000.0
NORM_EPS = 1e-06

HEAD = 128
HEADS = 8
ROWS = 768
NZ = 8
GROUP = 320
DEPTH = 2 * GROUP
COLS = 640
TILE = 256
TILES = ROWS // TILE
LONGEST = 384
QBLOCK = 128
TENSOR = ("y", "xl")
UP = [(z * 2 + c, (z + (1 - 2 * c)) % NZ * 2 + c) for z in range(NZ) for c in range(2)]
DOWN = [(target, source) for source, target in UP]
SWAP = [(0, 1), (1, 0)]

ANYWHERE = pl.BlockSpec(memory_space=pl.ANY)
VMEM = pl.BlockSpec(memory_space=pltpu.VMEM)
SMEM = pl.BlockSpec(memory_space=pltpu.SMEM)


def request_starts(length_row):
    ending = jnp.cumsum(length_row)
    offsets = ending - length_row
    row_ids = jnp.arange(ROWS, dtype=jnp.int32)
    reached = offsets[None, :] <= row_ids[:, None]
    return jnp.max(jnp.where(reached, offsets[None, :], 0), axis=1)


def rotary_tables(request_start):
    positions = (jnp.arange(ROWS, dtype=jnp.int32) - request_start).astype(jnp.float32)
    half = HEAD // 2
    frequency = ROPE_BASE ** (-jnp.arange(half, dtype=jnp.float32) * 2.0 / HEAD)
    angles = positions[:, None] * frequency[None, :]
    cosine, sine = jnp.cos(angles), jnp.sin(angles)
    return jnp.concatenate([cosine, cosine], axis=1), jnp.concatenate([-sine, sine], axis=1)


def regroup(weight):
    rows, groups, wide = weight.shape[0], 8, COLS - HEAD

    def kernel(weight_ref, out_ref):
        for core in range(2):
            for group in range(groups):
                index = core * groups + group
                first = (HEADS + core) * HEADS * HEAD + group * HEAD
                out_ref[index, :, :HEAD] = weight_ref[:, first : first + HEAD]
                first = (group * 2 + core) * wide
                out_ref[index, :, HEAD:] = weight_ref[:, first : first + wide]

    return pl.pallas_call(
        kernel,
        out_shape=jax.ShapeDtypeStruct((2 * groups, rows, COLS), weight.dtype),
        in_specs=[VMEM],
        out_specs=VMEM,
        compiler_params=pltpu.CompilerParams(vmem_limit_bytes=8 << 20),
        name="regroup",
    )(weight)


def gather_blocks(place, block, ahead):
    def up(array):
        return lax.ppermute(array, ("z", "c"), UP)

    def down(array):
        return lax.ppermute(array, ("z", "c"), DOWN)

    def across(array):
        return lax.ppermute(array, "xh", SWAP)

    other = across(block)
    up1, down1 = up(block), down(block)
    held, other_held, *tables = ahead
    up1, down1, held, tables = lax.optimization_barrier((up1, down1, held, tables))
    ahead = (held, other_held, *tables)
    held = ahead[:2]
    up2, down2 = up(up1), down(down1)
    up1, other = lax.optimization_barrier((up1, other))
    other_down1 = down(other)
    other_up1 = across(up1)
    totals = project_early(place, [(block, 0, 0, 0), (other, 0, 1, 0)], held)
    up2, down2, totals = lax.optimization_barrier((up2, down2, totals))
    up3, down3 = up(up2), down(down2)
    other_down2 = across(down2)
    other_up2 = up(other_up1)
    nearest = [
        (up1, -1, 0, 0), (other_up1, -1, 1, 0), (down1, 1, 0, 0), (other_down1, 1, 1, 0),
    ]
    totals = project_early(place, nearest, held, totals)
    up3, down3, totals = lax.optimization_barrier((up3, down3, totals))
    down4 = down(down3)
    other_down3 = across(down3)
    other_up3 = up(other_up2)
    second = [
        (up2, -2, 0, 0), (other_up2, -2, 1, 0), (down2, 2, 0, 0), (other_down2, 2, 1, 0),
    ]
    totals = project_early(place, second, held, totals)
    other_down3, totals = lax.optimization_barrier((other_down3, totals))
    other_down4 = down(other_down3)
    third = [
        (up3, -3, 0, 0), (other_up3, -3, 1, 0), (down3, 3, 0, 0), (other_down3, 3, 1, 0),
    ]
    totals = project_early(place, third, held, totals)
    last = [(down4, 4, 0, 0), (other_down4, 4, 1, 0)]
    return last, totals, ahead


def slots_of(pieces):
    offsets = []
    for _, offset, _, _ in pieces:
        if offset not in offsets:
            offsets.append(offset)
    return offsets


def assemble(place_ref, pieces, sources, target, wanted):
    offsets = slots_of(pieces)
    for (array, offset, flip, first), source in zip(pieces, sources):
        if offsets.index(offset) == wanted:
            side = lax.rem(place_ref[1] + flip, 2)
            row = pl.multiple_of(side * GROUP + (wanted * DEPTH + first), 16)
            target[pl.ds(row, array.shape[0])] = source[...]


def slot_of(offset):
    return (offset + NZ) % NZ


def hold_tokens(place, tokens):
    def kernel(place_ref, token_ref, out_ref, sems):
        z, core = place_ref[0], place_ref[2]
        wheres = [
            lax.rem(z + jnp.where(core == 0, slot, (NZ - slot) % NZ), NZ) for slot in range(NZ)
        ]
        copies = [
            pltpu.make_async_copy(
                token_ref.at[:, pl.ds(pl.multiple_of(wheres[slot] * DEPTH, HEAD), DEPTH)],
                out_ref.at[slot],
                sems.at[slot],
            )
            for slot in range(NZ)
        ]
        for copy in copies:
            copy.start()
        for copy in copies:
            copy.wait()

    return pl.pallas_call(
        kernel,
        out_shape=pltpu.VMEM((NZ, ROWS, DEPTH), jnp.bfloat16),
        in_specs=[SMEM, ANYWHERE],
        out_specs=ANYWHERE,
        scratch_shapes=[pltpu.SemaphoreType.DMA((NZ,))],
        compiler_params=pltpu.CompilerParams(vmem_limit_bytes=4 << 20),
        cost_estimate=pl.CostEstimate(flops=0, bytes_accessed=16 << 20, transcendentals=0),
        name="hold_tokens",
    )(place, pltpu.with_memory_space_constraint(tokens, pltpu.HBM))


def project_early(place, pieces, held_sets, totals=()):
    offsets = slots_of(pieces)
    count = len(offsets)

    def kernel(place_ref, *refs):
        sources, held_refs = refs[: len(pieces)], refs[len(pieces) : len(pieces) + 2]
        total_refs, out_refs, weight = refs[len(pieces) + 2 : -3], refs[-3:-1], refs[-1]
        for slot in range(count):
            assemble(place_ref, pieces, sources, weight, slot)
        for which, (held_ref, out_ref) in enumerate(zip(held_refs, out_refs)):
            for tile in range(TILES):
                rows = pl.ds(tile * TILE, TILE)
                part = jnp.concatenate(
                    [held_ref[slot_of(offset), rows] for offset in offsets], axis=1
                )
                product = jnp.dot(part, weight[...], preferred_element_type=jnp.float32)
                out_ref[rows] = total_refs[which][rows] + product if total_refs else product

    shape = pltpu.VMEM((ROWS, COLS), jnp.float32)
    return pl.pallas_call(
        kernel,
        out_shape=(shape, shape),
        in_specs=[SMEM] + [VMEM] * (len(pieces) + 2 + len(totals)),
        out_specs=(VMEM, VMEM),
        input_output_aliases={len(pieces) + 3 + which: which for which in range(len(totals))},
        scratch_shapes=[pltpu.VMEM((count * DEPTH, COLS), jnp.bfloat16)],
        compiler_params=pltpu.CompilerParams(vmem_limit_bytes=16 << 20),
        cost_estimate=pl.CostEstimate(
            flops=4 * ROWS * count * DEPTH * COLS, bytes_accessed=18 << 20, transcendentals=0
        ),
        name="project_early",
    )(place, *[piece[0] for piece in pieces], *held_sets, *totals)


def project_late(place, pieces, held, partial, cosine, sine, query_gain, key_gain, ready=None):
    offsets = slots_of(pieces)
    count = len(offsets)
    n_in = len(pieces) if ready is None else 1

    def kernel(place_ref, *refs):
        sources = refs[:n_in]
        held_ref, partial_ref, cos_ref, sin_ref, qgain_ref, kgain_ref, out_ref = refs[n_in : n_in + 7]
        core = place_ref[2]
        weight = refs[n_in + 7] if ready is None else sources[0]

        def normed(field, gain, rows):
            square = field * field
            upper = square.astype(jnp.bfloat16)
            lower = (square - upper.astype(jnp.float32)).astype(jnp.bfloat16)
            ones = jnp.ones((2 * HEAD, HEAD), jnp.bfloat16)
            total = jnp.dot(
                jnp.concatenate([upper, lower], axis=1), ones, preferred_element_type=jnp.float32
            )
            factor = lax.rsqrt(total * (1.0 / HEAD) + NORM_EPS)
            field = field * factor * gain
            return field * cos_ref[rows] + pltpu.roll(field, HEAD // 2, 1) * sin_ref[rows]

        for tile in range(TILES):
            rows = pl.ds(tile * TILE, TILE)
            result = partial_ref[rows]
            for slot, offset in enumerate(offsets):
                if tile == 0 and ready is None:
                    assemble(place_ref, pieces, sources, weight, slot)
                result = result + jnp.dot(
                    held_ref[slot_of(offset), rows],
                    weight[slot * DEPTH : (slot + 1) * DEPTH],
                    preferred_element_type=jnp.float32,
                )
            raw = result[:, :HEAD]
            key = normed(raw, kgain_ref[...], rows)
            out_ref[rows, :HEAD] = jnp.where(core == 0, key, raw).astype(jnp.bfloat16)
            for first in range(HEAD, COLS, HEAD):
                field = normed(result[:, first : first + HEAD], qgain_ref[...], rows)
                out_ref[rows, first : first + HEAD] = field.astype(jnp.bfloat16)

    shape = jax.ShapeDtypeStruct((ROWS, COLS), jnp.bfloat16)
    weight_shape = pltpu.VMEM((count * DEPTH, COLS), jnp.bfloat16)
    first = ready is None
    return pl.pallas_call(
        kernel,
        out_shape=(shape, weight_shape) if first else shape,
        in_specs=[SMEM] + [VMEM] * (n_in + 6),
        out_specs=(VMEM, VMEM) if first else VMEM,
        compiler_params=pltpu.CompilerParams(vmem_limit_bytes=16 << 20),
        cost_estimate=pl.CostEstimate(
            flops=2 * ROWS * count * DEPTH * COLS, bytes_accessed=9 << 20, transcendentals=0
        ),
        name="project_late",
    )(
        place, *([piece[0] for piece in pieces] if first else [ready]), held, partial, cosine, sine,
        query_gain, key_gain,
    )


def attend(place, own, received, request_start):
    scale = math.log2(math.e) / math.sqrt(HEAD)

    def kernel(place_ref, own_ref, received_ref, start_ref, out_hbm, key_ref, value_ref, out_ref, sems):
        core = place_ref[2]

        def written(block):
            rows = pl.ds(block * QBLOCK, QBLOCK)
            return pltpu.make_async_copy(out_ref.at[rows], out_hbm.at[rows], sems.at[block])

        key_ref[...] = jnp.where(core == 0, own_ref[:, :HEAD], received_ref[:, :HEAD])
        value_ref[:, :HEAD] = jnp.where(core == 0, received_ref[:, :HEAD], own_ref[:, :HEAD])
        value_ref[:, HEAD:] = jnp.ones((ROWS, HEAD), jnp.bfloat16)
        for block in range(ROWS // QBLOCK):
            rows = pl.ds(block * QBLOCK, QBLOCK)
            low = max(0, block * QBLOCK - LONGEST + 1) // QBLOCK * QBLOCK
            count = (block + 1) * QBLOCK - low
            keys, values = key_ref[pl.ds(low, count)], value_ref[pl.ds(low, count)]
            row_ids = block * QBLOCK + lax.broadcasted_iota(jnp.int32, (QBLOCK, count), 0)
            key_ids = low + lax.broadcasted_iota(jnp.int32, (QBLOCK, count), 1)
            allowed = (key_ids <= row_ids) & (key_ids >= start_ref[rows])
            bias = jnp.where(allowed, 0.0, -1e30)
            for side, source in enumerate((own_ref, received_ref)):
                first = pl.multiple_of((core if side == 0 else 1 - core) * 512, 512)
                queries = jnp.concatenate(
                    [source[rows, head * HEAD : (head + 1) * HEAD] for head in range(1, 5)], axis=0
                )
                scores = lax.dot_general(
                    queries, keys, (((1,), (1,)), ((), ())), preferred_element_type=jnp.float32
                )
                scores = (scores.reshape(4, QBLOCK, count) + bias[None]).reshape(4 * QBLOCK, count)
                top = jnp.max(scores, axis=1, keepdims=True)
                weights = jnp.exp2((scores - top) * scale).astype(jnp.bfloat16)
                mixed = jnp.dot(weights, values, preferred_element_type=jnp.float32)
                mixed = (mixed[:, :HEAD] / mixed[:, HEAD:]).astype(jnp.bfloat16)
                for head in range(4):
                    out_ref[rows, pl.ds(first + head * HEAD, HEAD)] = mixed[
                        head * QBLOCK : (head + 1) * QBLOCK
                    ]
            written(block).start()
        for block in range(ROWS // QBLOCK):
            written(block).wait()

    return pl.pallas_call(
        kernel,
        out_shape=jax.ShapeDtypeStruct((ROWS, 8 * HEAD), jnp.bfloat16),
        in_specs=[SMEM, VMEM, VMEM, VMEM],
        out_specs=ANYWHERE,
        scratch_shapes=[
            pltpu.VMEM((ROWS, HEAD), jnp.bfloat16),
            pltpu.VMEM((ROWS, 2 * HEAD), jnp.bfloat16),
            pltpu.VMEM((ROWS, HEADS * HEAD), jnp.bfloat16),
            pltpu.SemaphoreType.DMA((ROWS // QBLOCK,)),
        ],
        compiler_params=pltpu.CompilerParams(vmem_limit_bytes=32 << 20),
        cost_estimate=pl.CostEstimate(
            flops=4 * 8 * ROWS * 512 * HEAD, bytes_accessed=4 << 20, transcendentals=8 * ROWS * 512
        ),
        name="attend",
    )(place, own, received, request_start)


def shards(tokens, lengths, qkv_weight, query_norm_gain, key_norm_gain):
    place = jnp.stack([lax.axis_index("z"), lax.axis_index("xh"), lax.axis_index("c")]).astype(
        jnp.int32
    )
    other_tokens = lax.ppermute(tokens, "c", SWAP)
    other_lengths = lax.ppermute(lengths, "c", SWAP)
    spread = regroup(qkv_weight)
    block = lax.all_to_all(spread, ("c",) + TENSOR, split_axis=0, concat_axis=0, tiled=True)
    own_start, other_start = request_starts(lengths[0]), request_starts(other_lengths[0])
    own_tables, other_tables = rotary_tables(own_start), rotary_tables(other_start)
    block, own_tables, other_tables = lax.optimization_barrier((block, own_tables, other_tables))
    held = hold_tokens(place, tokens)
    other_held = hold_tokens(place, other_tokens)
    late, totals, ahead = gather_blocks(
        place, block.reshape(GROUP, COLS), (held, other_held, *own_tables, *other_tables)
    )
    held, other_held, *tables = ahead
    own_tables, other_tables = tables[:2], tables[2:]
    gains = (query_norm_gain.reshape(1, HEAD), key_norm_gain.reshape(1, HEAD))
    own_partial, other_partial = totals
    other, ready = project_late(place, late, other_held, other_partial, *other_tables, *gains)
    received = lax.ppermute(other, "c", SWAP)
    own = project_late(place, late, held, own_partial, *own_tables, *gains, ready)
    return attend(place, own, received, own_start.reshape(ROWS, 1))


def solution(mesh):
    fine = Mesh(mesh.devices.reshape(NZ, 2, 2, 4, 2), ("z", "xh", "c") + TENSOR)
    rows = ("z", "xh", "c")
    in_specs = (P(rows, None), P(rows, None), P(rows + TENSOR, None), P(), P())
    return jax.shard_map(
        shards, mesh=fine, in_specs=in_specs, out_specs=P(rows, TENSOR), check_vma=False
    )
```

```python
import math

import jax
import jax.numpy as jnp
from jax import lax
from jax.experimental import pallas as pl
from jax.experimental.pallas import tpu as pltpu
from jax.sharding import Mesh, PartitionSpec as P

ROPE_BASE = 1000000.0
NORM_EPS = 1e-06

HEAD = 128
HEADS = 8
ROWS = 768
NZ = 8
GROUP = 320
DEPTH = 2 * GROUP
COLS = 640
TILE = 256
TILES = ROWS // TILE
LONGEST = 384
QBLOCK = 128
TENSOR = ("y", "xl")
UP = [(z * 2 + c, (z + (1 - 2 * c)) % NZ * 2 + c) for z in range(NZ) for c in range(2)]
DOWN = [(target, source) for source, target in UP]
SWAP = [(0, 1), (1, 0)]

ANYWHERE = pl.BlockSpec(memory_space=pl.ANY)
VMEM = pl.BlockSpec(memory_space=pltpu.VMEM)
SMEM = pl.BlockSpec(memory_space=pltpu.SMEM)


def request_starts(length_row):
    ending = jnp.cumsum(length_row)
    offsets = ending - length_row
    row_ids = jnp.arange(ROWS, dtype=jnp.int32)
    reached = offsets[None, :] <= row_ids[:, None]
    return jnp.max(jnp.where(reached, offsets[None, :], 0), axis=1)


def rotary_tables(request_start):
    positions = (jnp.arange(ROWS, dtype=jnp.int32) - request_start).astype(jnp.float32)
    half = HEAD // 2
    frequency = ROPE_BASE ** (-jnp.arange(half, dtype=jnp.float32) * 2.0 / HEAD)
    angles = positions[:, None] * frequency[None, :]
    cosine, sine = jnp.cos(angles), jnp.sin(angles)
    return jnp.concatenate([cosine, cosine], axis=1), jnp.concatenate([-sine, sine], axis=1)


def regroup(weight):
    rows, groups, wide = weight.shape[0], 8, COLS - HEAD

    def kernel(weight_ref, out_ref):
        for core in range(2):
            for group in range(groups):
                index = core * groups + group
                first = (HEADS + core) * HEADS * HEAD + group * HEAD
                out_ref[index, :, :HEAD] = weight_ref[:, first : first + HEAD]
                first = (group * 2 + core) * wide
                out_ref[index, :, HEAD:] = weight_ref[:, first : first + wide]

    return pl.pallas_call(
        kernel,
        out_shape=jax.ShapeDtypeStruct((2 * groups, rows, COLS), weight.dtype),
        in_specs=[VMEM],
        out_specs=VMEM,
        compiler_params=pltpu.CompilerParams(vmem_limit_bytes=8 << 20),
        name="regroup",
    )(weight)


def gather_blocks(place, block, ahead):
    def up(array):
        return lax.ppermute(array, ("z", "c"), UP)

    def down(array):
        return lax.ppermute(array, ("z", "c"), DOWN)

    def across(array):
        return lax.ppermute(array, "xh", SWAP)

    other = across(block)
    up1, down1 = up(block), down(block)
    held, other_held, *tables = ahead
    up1, down1, held, tables = lax.optimization_barrier((up1, down1, held, tables))
    ahead = (held, other_held, *tables)
    held = ahead[:2]
    up2, down2 = up(up1), down(down1)
    up1, other = lax.optimization_barrier((up1, other))
    other_down1 = down(other)
    other_up1 = across(up1)
    totals = project_early(place, [(block, 0, 0, 0), (other, 0, 1, 0)], held)
    up2, down2, totals = lax.optimization_barrier((up2, down2, totals))
    up3, down3 = up(up2), down(down2)
    other_down2 = across(down2)
    other_up2 = up(other_up1)
    nearest = [
        (up1, -1, 0, 0), (other_up1, -1, 1, 0), (down1, 1, 0, 0), (other_down1, 1, 1, 0),
    ]
    totals = project_early(place, nearest, held, totals)
    up3, down3, totals = lax.optimization_barrier((up3, down3, totals))
    up4 = up(up3)
    other_down3 = across(down3)
    other_up3 = up(other_up2)
    second = [
        (up2, -2, 0, 0), (other_up2, -2, 1, 0), (down2, 2, 0, 0), (other_down2, 2, 1, 0),
    ]
    totals = project_early(place, second, held, totals)
    other_down3, totals = lax.optimization_barrier((other_down3, totals))
    other_down4 = down(other_down3)
    third = [
        (up3, -3, 0, 0), (other_up3, -3, 1, 0), (down3, 3, 0, 0), (other_down3, 3, 1, 0),
    ]
    totals = project_early(place, third, held, totals)
    last = [(up4, 4, 0, 0), (other_down4, 4, 1, 0)]
    return last, totals, ahead


def slots_of(pieces):
    offsets = []
    for _, offset, _, _ in pieces:
        if offset not in offsets:
            offsets.append(offset)
    return offsets


def assemble(place_ref, pieces, sources, target, wanted):
    offsets = slots_of(pieces)
    for (array, offset, flip, first), source in zip(pieces, sources):
        if offsets.index(offset) == wanted:
            side = lax.rem(place_ref[1] + flip, 2)
            row = pl.multiple_of(side * GROUP + (wanted * DEPTH + first), 16)
            target[pl.ds(row, array.shape[0])] = source[...]


def slot_of(offset):
    return (offset + NZ) % NZ


def hold_tokens(place, tokens):
    def kernel(place_ref, token_ref, out_ref, sems):
        z, core = place_ref[0], place_ref[2]
        wheres = [
            lax.rem(z + jnp.where(core == 0, slot, (NZ - slot) % NZ), NZ) for slot in range(NZ)
        ]
        copies = [
            pltpu.make_async_copy(
                token_ref.at[:, pl.ds(pl.multiple_of(wheres[slot] * DEPTH, HEAD), DEPTH)],
                out_ref.at[slot],
                sems.at[slot],
            )
            for slot in range(NZ)
        ]
        for copy in copies:
            copy.start()
        for copy in copies:
            copy.wait()

    return pl.pallas_call(
        kernel,
        out_shape=pltpu.VMEM((NZ, ROWS, DEPTH), jnp.bfloat16),
        in_specs=[SMEM, ANYWHERE],
        out_specs=ANYWHERE,
        scratch_shapes=[pltpu.SemaphoreType.DMA((NZ,))],
        compiler_params=pltpu.CompilerParams(vmem_limit_bytes=4 << 20),
        cost_estimate=pl.CostEstimate(flops=0, bytes_accessed=16 << 20, transcendentals=0),
        name="hold_tokens",
    )(place, pltpu.with_memory_space_constraint(tokens, pltpu.HBM))


def project_early(place, pieces, held_sets, totals=()):
    offsets = slots_of(pieces)
    count = len(offsets)

    def kernel(place_ref, *refs):
        sources, held_refs = refs[: len(pieces)], refs[len(pieces) : len(pieces) + 2]
        total_refs, out_refs, weight = refs[len(pieces) + 2 : -3], refs[-3:-1], refs[-1]
        for slot in range(count):
            assemble(place_ref, pieces, sources, weight, slot)
        for which, (held_ref, out_ref) in enumerate(zip(held_refs, out_refs)):
            for tile in range(TILES):
                rows = pl.ds(tile * TILE, TILE)
                part = jnp.concatenate(
                    [held_ref[slot_of(offset), rows] for offset in offsets], axis=1
                )
                product = jnp.dot(part, weight[...], preferred_element_type=jnp.float32)
                out_ref[rows] = total_refs[which][rows] + product if total_refs else product

    shape = pltpu.VMEM((ROWS, COLS), jnp.float32)
    return pl.pallas_call(
        kernel,
        out_shape=(shape, shape),
        in_specs=[SMEM] + [VMEM] * (len(pieces) + 2 + len(totals)),
        out_specs=(VMEM, VMEM),
        input_output_aliases={len(pieces) + 3 + which: which for which in range(len(totals))},
        scratch_shapes=[pltpu.VMEM((count * DEPTH, COLS), jnp.bfloat16)],
        compiler_params=pltpu.CompilerParams(vmem_limit_bytes=16 << 20),
        cost_estimate=pl.CostEstimate(
            flops=4 * ROWS * count * DEPTH * COLS, bytes_accessed=18 << 20, transcendentals=0
        ),
        name="project_early",
    )(place, *[piece[0] for piece in pieces], *held_sets, *totals)


def project_late(place, pieces, held, partial, cosine, sine, query_gain, key_gain, ready=None):
    offsets = slots_of(pieces)
    count = len(offsets)
    n_in = len(pieces) if ready is None else 1

    def kernel(place_ref, *refs):
        sources = refs[:n_in]
        held_ref, partial_ref, cos_ref, sin_ref, qgain_ref, kgain_ref, out_ref = refs[n_in : n_in + 7]
        core = place_ref[2]
        weight = refs[n_in + 7] if ready is None else sources[0]

        def normed(field, gain, rows):
            square = field * field
            upper = square.astype(jnp.bfloat16)
            lower = (square - upper.astype(jnp.float32)).astype(jnp.bfloat16)
            ones = jnp.ones((2 * HEAD, HEAD), jnp.bfloat16)
            total = jnp.dot(
                jnp.concatenate([upper, lower], axis=1), ones, preferred_element_type=jnp.float32
            )
            factor = lax.rsqrt(total * (1.0 / HEAD) + NORM_EPS)
            field = field * factor * gain
            return field * cos_ref[rows] + pltpu.roll(field, HEAD // 2, 1) * sin_ref[rows]

        for tile in range(TILES):
            rows = pl.ds(tile * TILE, TILE)
            result = partial_ref[rows]
            for slot, offset in enumerate(offsets):
                if tile == 0 and ready is None:
                    assemble(place_ref, pieces, sources, weight, slot)
                result = result + jnp.dot(
                    held_ref[slot_of(offset), rows],
                    weight[slot * DEPTH : (slot + 1) * DEPTH],
                    preferred_element_type=jnp.float32,
                )
            raw = result[:, :HEAD]
            key = normed(raw, kgain_ref[...], rows)
            out_ref[rows, :HEAD] = jnp.where(core == 0, key, raw).astype(jnp.bfloat16)
            for first in range(HEAD, COLS, HEAD):
                field = normed(result[:, first : first + HEAD], qgain_ref[...], rows)
                out_ref[rows, first : first + HEAD] = field.astype(jnp.bfloat16)

    shape = jax.ShapeDtypeStruct((ROWS, COLS), jnp.bfloat16)
    weight_shape = pltpu.VMEM((count * DEPTH, COLS), jnp.bfloat16)
    first = ready is None
    return pl.pallas_call(
        kernel,
        out_shape=(shape, weight_shape) if first else shape,
        in_specs=[SMEM] + [VMEM] * (n_in + 6),
        out_specs=(VMEM, VMEM) if first else VMEM,
        compiler_params=pltpu.CompilerParams(vmem_limit_bytes=16 << 20),
        cost_estimate=pl.CostEstimate(
            flops=2 * ROWS * count * DEPTH * COLS, bytes_accessed=9 << 20, transcendentals=0
        ),
        name="project_late",
    )(
        place, *([piece[0] for piece in pieces] if first else [ready]), held, partial, cosine, sine,
        query_gain, key_gain,
    )


def attend(place, own, received, request_start):
    scale = math.log2(math.e) / math.sqrt(HEAD)

    def kernel(place_ref, own_ref, received_ref, start_ref, out_hbm, key_ref, value_ref, out_ref, sems):
        core = place_ref[2]

        def written(block):
            rows = pl.ds(block * QBLOCK, QBLOCK)
            return pltpu.make_async_copy(out_ref.at[rows], out_hbm.at[rows], sems.at[block])

        key_ref[...] = jnp.where(core == 0, own_ref[:, :HEAD], received_ref[:, :HEAD])
        value_ref[:, :HEAD] = jnp.where(core == 0, received_ref[:, :HEAD], own_ref[:, :HEAD])
        value_ref[:, HEAD:] = jnp.ones((ROWS, HEAD), jnp.bfloat16)
        for block in range(ROWS // QBLOCK):
            rows = pl.ds(block * QBLOCK, QBLOCK)
            low = max(0, block * QBLOCK - LONGEST + 1) // QBLOCK * QBLOCK
            count = (block + 1) * QBLOCK - low
            keys, values = key_ref[pl.ds(low, count)], value_ref[pl.ds(low, count)]
            row_ids = block * QBLOCK + lax.broadcasted_iota(jnp.int32, (QBLOCK, count), 0)
            key_ids = low + lax.broadcasted_iota(jnp.int32, (QBLOCK, count), 1)
            allowed = (key_ids <= row_ids) & (key_ids >= start_ref[rows])
            bias = jnp.where(allowed, 0.0, -1e30)
            for side, source in enumerate((own_ref, received_ref)):
                first = pl.multiple_of((core if side == 0 else 1 - core) * 512, 512)
                queries = jnp.concatenate(
                    [source[rows, head * HEAD : (head + 1) * HEAD] for head in range(1, 5)], axis=0
                )
                scores = lax.dot_general(
                    queries, keys, (((1,), (1,)), ((), ())), preferred_element_type=jnp.float32
                )
                scores = (scores.reshape(4, QBLOCK, count) + bias[None]).reshape(4 * QBLOCK, count)
                top = jnp.max(scores, axis=1, keepdims=True)
                weights = jnp.exp2((scores - top) * scale).astype(jnp.bfloat16)
                mixed = jnp.dot(weights, values, preferred_element_type=jnp.float32)
                mixed = (mixed[:, :HEAD] / mixed[:, HEAD:]).astype(jnp.bfloat16)
                for head in range(4):
                    out_ref[rows, pl.ds(first + head * HEAD, HEAD)] = mixed[
                        head * QBLOCK : (head + 1) * QBLOCK
                    ]
            written(block).start()
        for block in range(ROWS // QBLOCK):
            written(block).wait()

    return pl.pallas_call(
        kernel,
        out_shape=jax.ShapeDtypeStruct((ROWS, 8 * HEAD), jnp.bfloat16),
        in_specs=[SMEM, VMEM, VMEM, VMEM],
        out_specs=ANYWHERE,
        scratch_shapes=[
            pltpu.VMEM((ROWS, HEAD), jnp.bfloat16),
            pltpu.VMEM((ROWS, 2 * HEAD), jnp.bfloat16),
            pltpu.VMEM((ROWS, HEADS * HEAD), jnp.bfloat16),
            pltpu.SemaphoreType.DMA((ROWS // QBLOCK,)),
        ],
        compiler_params=pltpu.CompilerParams(vmem_limit_bytes=32 << 20),
        cost_estimate=pl.CostEstimate(
            flops=4 * 8 * ROWS * 512 * HEAD, bytes_accessed=4 << 20, transcendentals=8 * ROWS * 512
        ),
        name="attend",
    )(place, own, received, request_start)


def shards(tokens, lengths, qkv_weight, query_norm_gain, key_norm_gain):
    place = jnp.stack([lax.axis_index("z"), lax.axis_index("xh"), lax.axis_index("c")]).astype(
        jnp.int32
    )
    other_tokens = lax.ppermute(tokens, "c", SWAP)
    other_lengths = lax.ppermute(lengths, "c", SWAP)
    spread = regroup(qkv_weight)
    block = lax.all_to_all(spread, ("c",) + TENSOR, split_axis=0, concat_axis=0, tiled=True)
    own_start, other_start = request_starts(lengths[0]), request_starts(other_lengths[0])
    own_tables, other_tables = rotary_tables(own_start), rotary_tables(other_start)
    block, own_tables, other_tables = lax.optimization_barrier((block, own_tables, other_tables))
    held = hold_tokens(place, tokens)
    other_held = hold_tokens(place, other_tokens)
    late, totals, ahead = gather_blocks(
        place, block.reshape(GROUP, COLS), (held, other_held, *own_tables, *other_tables)
    )
    held, other_held, *tables = ahead
    own_tables, other_tables = tables[:2], tables[2:]
    gains = (query_norm_gain.reshape(1, HEAD), key_norm_gain.reshape(1, HEAD))
    own_partial, other_partial = totals
    other, ready = project_late(place, late, other_held, other_partial, *other_tables, *gains)
    received = lax.ppermute(other, "c", SWAP)
    own = project_late(place, late, held, own_partial, *own_tables, *gains, ready)
    return attend(place, own, received, own_start.reshape(ROWS, 1))


def solution(mesh):
    fine = Mesh(mesh.devices.reshape(NZ, 2, 2, 4, 2), ("z", "xh", "c") + TENSOR)
    rows = ("z", "xh", "c")
    in_specs = (P(rows, None), P(rows, None), P(rows + TENSOR, None), P(), P())
    return jax.shard_map(
        shards, mesh=fine, in_specs=in_specs, out_specs=P(rows, TENSOR), check_vma=False
    )
```
